32 devices in a mesh: ctx: 8 (over y, x, core), exp: 4 (over z).
Axes of the slice: x: 2, y: 2, z: 4, core: 2. Of those that a mesh axis runs over, the one named last changes fastest.
Arguments:
- queries: bfloat16 [4, 512, 8192], P(None, 'ctx', 'exp'), may hold values from -2 to 2
- keys: bfloat16 [4, 512, 8192], P(None, 'ctx', 'exp'), may hold values from -2 to 2
- values: bfloat16 [4, 512, 8192], P(None, 'ctx', 'exp'), may hold values from -6 to 6
- decay_log: float32 [512, 64], P('ctx', 'exp'), may hold values from -0.9 to 0
- out_gate: bfloat16 [4, 512, 8192], P(None, 'ctx', 'exp'), may hold values from -6 to 6
- head_gain: float32 [8192], P('exp'), may hold values from 0.1 to 1.9
- out_weight: bfloat16 [8192, 6144], P('exp', 'ctx'), may hold values from -0.0625 to 0.0625
- stream: bfloat16 [4, 512, 6144], P(None, ('ctx', 'exp')), may hold values from -6 to 6
- norm_gain: float32 [6144], replicated, may hold values from 0.1 to 1.9
- expert_ids: int32 [32, 64, 2], P(('ctx', 'exp')), may hold values from 0 to 3, all different within a row; in each aligned block of 64 rows (0 to 63, 64 to 127, ..., all dimensions but the last counted through in order) at most 33 rows name the same one
- expert_share: float32 [32, 64, 2], P(('ctx', 'exp')), may hold values from 0.2 to 1
- w_gate: bfloat16 [4, 6144, 9216], P('exp', None, 'ctx'), may hold values from -0.078125 to 0.078125
- w_up: bfloat16 [4, 6144, 9216], P('exp', None, 'ctx'), may hold values from -0.078125 to 0.078125
- w_down: bfloat16 [4, 9216, 6144], P('exp', 'ctx'), may hold values from -0.0625 to 0.0625
Outputs:
- layer_out: bfloat16 [4, 512, 6144], P(None, ('ctx', 'exp'))
The draws below stay inside these ranges and needn't reach their ends.
Inputs may be any that keep to these rules, and one draw needn't show every extreme that they name: `expert_ids`: within a routing group no expert takes more than 33 copies, some group gives one expert exactly 33, and the two picks of a token differ.
All inputs are finite; a program needn't handle non-finite values.
Results may differ from the reference program's by a relative error of at most 0.02.
Values may be sent and summed in bfloat16 or wider, within the bound.
No kernel may reach another device: no remote copies, remote signals or barrier semaphores. Data moves between devices by JAX's collectives and lax.ppermute only.
A program may use at most 192 MiB of HBM per device.

```python
import math
import jax
import jax.numpy as jnp
import numpy as np
from jax import lax

D = 6144
HEAD_TOTAL = 64
HD = 128
HID = 9216
SEQS = 4
BLOCK = 64
SEQUENCE_LENGTH = 512
SUB = 16
TOK_DEV = 64
GROUPS = 32
HID_DEV = 1152
EXPERTS = 4
MOST = 33
N_CTX = 8


def draw_decay_log(key, part):
    every_key_row = jax.random.split(key, 6)
    fast_share = 0.5
    chooser = jax.random.uniform(every_key_row[0], (HEAD_TOTAL,))
    fast_rate = jnp.exp(jax.random.uniform(every_key_row[1], (HEAD_TOTAL,), minval=math.log(1.0 / 50.0), maxval=math.log(1.0 / 30.0)))
    slow_rate = jnp.exp(jax.random.uniform(every_key_row[2], (HEAD_TOTAL,), minval=math.log(0.05 / SEQUENCE_LENGTH), maxval=math.log(0.5 / SEQUENCE_LENGTH)))
    baseline_decay_rate = jnp.where(chooser < fast_share, fast_rate, slow_rate)
    jitter_amplitude = jnp.exp(jax.random.uniform(every_key_row[3], (SEQUENCE_LENGTH, HEAD_TOTAL), minval=math.log(0.5), maxval=math.log(2.0)))
    spike_positions = jax.random.randint(every_key_row[4], (3,), 0, SEQUENCE_LENGTH)
    spike_flags = jnp.any(jnp.arange(SEQUENCE_LENGTH)[:, None] == spike_positions[None, :], axis=1)
    spike_magnitude = jax.random.uniform(every_key_row[5], (SEQUENCE_LENGTH, HEAD_TOTAL), minval=math.log(0.5), maxval=math.log(0.8))
    decay_result = -baseline_decay_rate[None, :] * jitter_amplitude + jnp.where(spike_flags[:, None], spike_magnitude, 0.0)
    return decay_result.astype(jnp.float32)


def shard_levels(stream_key, dims, shards, least, top_value):
    def one(dim, blocks):
        draws = jax.random.uniform(jax.random.fold_in(jax.random.fold_in(stream_key, 6), dim), (blocks,), jnp.float32, least / len(shards), top_value / len(shards))
        return jnp.repeat(jnp.exp(draws), dims[dim] // blocks).reshape((-1,) + (1,) * (len(dims) - dim - 1))

    level = one(*shards[0])
    for cut in shards[1:]:
        level = level * one(*cut)
    return level


def routed_block(own_key, own, number, rows, amount, top, most, slope):
    order = jax.random.permutation(own_key, amount)
    crowded, usual = portions_of(amount, rows * top, most, slope, True), portions_of(amount, rows * top, most, slope, False)
    places = jnp.arange(amount)

    def named(tallies, offset_by):
        used = int((tallies > 0).sum())
        fixed = max(1, used // 4)
        passed = fixed + (places - fixed + offset_by * (used - fixed)) % max(1, amount - fixed)
        return jnp.zeros((amount,), jnp.int32).at[order[jnp.where(places < fixed, places, passed)]].set(jnp.asarray(tallies, jnp.int32))

    tallies = jnp.where(number % 4 == 0, named(crowded, number // 4), named(usual, number - number // 4 - 1))
    mixed = jax.random.permutation(jax.random.fold_in(own, 3), amount)
    donor, sink = mixed[0:amount // 2 * 2:2], mixed[1:amount // 2 * 2:2]
    slack = jnp.minimum(tallies[donor] - 1, most - tallies[sink]) // 2
    slack = jnp.where((donor == order[0]) | (sink == order[0]) | (tallies[sink] == 0), 0, jnp.maximum(slack, 0))
    passed = jax.random.randint(jax.random.fold_in(own, 4), (amount // 2,), 0, 1 << 20) % (slack + 1)
    tallies = tallies.at[donor].add(-passed).at[sink].add(passed)
    members = jnp.searchsorted(jnp.cumsum(tallies), jnp.arange(rows * top), side="right").astype(jnp.int32)
    listing = members.reshape(top, rows).T
    listing = listing[jax.random.permutation(jax.random.fold_in(own, 1), rows)]
    offset_by = jax.random.randint(jax.random.fold_in(own, 2), (rows, 1), 0, top)
    return jnp.take_along_axis(listing, (jnp.arange(top)[None, :] + offset_by) % top, axis=1)


def portions_of(amount, total, bound, slope, full):
    loads = [(1 << 20) // math.isqrt(grade ** slope) + 1 for grade in range(1, amount + 1)]
    largest = bound if full else min(bound, max(-(-total // amount), total * loads[0] // sum(loads)))
    least = 1 if total - largest >= amount - 1 else 0
    given, surplus = [largest] + [least] * (amount - 1), total - largest - least * (amount - 1)
    while surplus > 0:
        movable = [i for i in range(1, amount) if given[i] < largest] or [i for i in range(1, amount) if given[i] < bound]
        pool, budget = sum([loads[i] for i in movable]), surplus
        for i in movable:
            extra = min(bound - given[i], max(1, budget * loads[i] // pool), surplus)
            given[i] = given[i] + extra
            surplus = surplus - extra
    return np.array(given)


def gaussian(rng, extent, deviation, limit, cuts=(), kind=jnp.bfloat16):
    entries = deviation * jax.random.normal(rng, extent, jnp.float32)
    if cuts:
        entries = entries * shard_levels(rng, extent, cuts, -0.22, 0.18)
    return jnp.clip(entries, -limit, limit).astype(kind)


def setup_inputs(seed: int = 0) -> dict:
    splits = jax.random.split(jax.random.key(seed), 15)
    queries = gaussian(splits[0], (SEQS, SEQUENCE_LENGTH, HEAD_TOTAL * HD), 0.35, 2.0, ((1, 8), (2, 4)))
    keys = gaussian(splits[1], (SEQS, SEQUENCE_LENGTH, HEAD_TOTAL * HD), 0.35, 2.0, ((1, 8), (2, 4)))
    values = gaussian(splits[2], (SEQS, SEQUENCE_LENGTH, HEAD_TOTAL * HD), 1.0, 6.0, ((1, 8), (2, 4)))
    decay_log = draw_decay_log(jax.random.fold_in(splits[14], 71), 0)
    out_gate = gaussian(splits[4], (SEQS, SEQUENCE_LENGTH, HEAD_TOTAL * HD), 1.0, 6.0, ((1, 8), (2, 4)))
    head_gain = jnp.clip(1.0 + 0.18 * jax.random.normal(splits[5], (HEAD_TOTAL * HD,), jnp.float32), 0.1, 1.9)
    out_weight = gaussian(splits[6], (HEAD_TOTAL * HD, D), (HEAD_TOTAL * HD) ** -0.5, 0.0625, ((0, 4), (1, 8)))
    stream = gaussian(splits[7], (SEQS, SEQUENCE_LENGTH, D), 1.0, 6.0, ((1, 32),))
    norm_gain = jnp.clip(1.0 + 0.18 * jax.random.normal(splits[8], (D,), jnp.float32), 0.1, 1.9)
    expert_ids_keys = jax.random.split(jax.random.fold_in(splits[9], 1), GROUPS * TOK_DEV // TOK_DEV)
    expert_ids_turns = jax.random.permutation(jax.random.fold_in(splits[9], 3), GROUPS * TOK_DEV // TOK_DEV)
    expert_ids = jax.vmap(lambda own, number: routed_block(jax.random.fold_in(splits[9], 2), own, number, TOK_DEV, EXPERTS, 2, MOST, 2))(expert_ids_keys, expert_ids_turns).reshape((GROUPS, TOK_DEV, 2))
    expert_share = jnp.clip(0.2 + 0.8 * jax.random.uniform(splits[10], (GROUPS, TOK_DEV, 2), jnp.float32) ** shard_levels(splits[10], (GROUPS, TOK_DEV, 2), ((0, 32),), -0.2, 0.2), 0.2, 1.0)
    w_gate = gaussian(splits[11], (EXPERTS, D, HID), D ** -0.5, 0.078125, ((0, 4), (2, 8)))
    w_up = gaussian(splits[12], (EXPERTS, D, HID), D ** -0.5, 0.078125, ((0, 4), (2, 8)))
    w_down = gaussian(splits[13], (EXPERTS, HID, D), HID ** -0.5, 0.0625, ((0, 4), (1, 8)))
    return dict(queries=queries, keys=keys, values=values, decay_log=decay_log, out_gate=out_gate, head_gain=head_gain, out_weight=out_weight, stream=stream, norm_gain=norm_gain, expert_ids=expert_ids, expert_share=expert_share, w_gate=w_gate, w_up=w_up, w_down=w_down)


def reference(queries, keys, values, decay_log, out_gate, head_gain, out_weight, stream, norm_gain, expert_ids, expert_share, w_gate, w_up, w_down):
    split_shape = (SEQS, N_CTX, BLOCK, HEAD_TOTAL, HD)
    query_all = queries.astype(jnp.float32).reshape(split_shape)
    key_all = keys.astype(jnp.float32).reshape(split_shape)
    value_all = values.astype(jnp.float32).reshape(split_shape)
    cumulative = jnp.cumsum(decay_log.reshape(N_CTX, BLOCK, HEAD_TOTAL), axis=1)
    position = jnp.arange(BLOCK)
    causal = position[:, None] >= position[None, :]
    gap_log = cumulative[:, :, None, :] - cumulative[:, None, :, :]
    decay_grid = jnp.exp(jnp.where(causal[None, :, :, None], gap_log, -1e+30))
    scores = jnp.einsum('sbihd,sbjhd->sbijh', query_all, key_all)
    weights = (scores * decay_grid[None]).astype(jnp.bfloat16)
    within = jnp.einsum('sbijh,sbjhd->sbihd', weights.astype(jnp.float32), value_all)
    block_end = cumulative[:, -1, :]
    keys_faded = jnp.exp(block_end[:, None, :] - cumulative)[None, :, :, :, None] * key_all
    local_state = jnp.einsum('sbjhd,sbjhe->sbhde', keys_faded, value_all, precision=lax.Precision.HIGHEST)
    fading = jnp.exp(block_end)

    def advance(state_in, inputs):
        fade_now, local_now = inputs
        return (fade_now[None, :, None, None] * state_in + local_now, state_in)
    start_state = jnp.zeros((SEQS, HEAD_TOTAL, HD, HD), jnp.float32)
    _, incoming = lax.scan(advance, start_state, (fading, jnp.moveaxis(local_state, 1, 0)))
    incoming = jnp.moveaxis(incoming, 0, 1)
    carried = jnp.exp(cumulative)[None, :, :, :, None] * jnp.einsum('sbihd,sbhde->sbihe', query_all, incoming, precision=lax.Precision.HIGHEST)
    attended = within + carried
    mean_square = lax.optimization_barrier(jnp.mean(attended * attended, axis=-1, keepdims=True))
    gate_act = jax.nn.sigmoid(out_gate.astype(jnp.float32).reshape(split_shape))
    gated = attended * lax.rsqrt(mean_square + 1e-06) * head_gain.reshape(HEAD_TOTAL, HD) * gate_act
    mixed = gated.astype(jnp.bfloat16).reshape(SEQS * SEQUENCE_LENGTH, HEAD_TOTAL * HD)
    residual_sum = stream.astype(jnp.float32).reshape(SEQS * SEQUENCE_LENGTH, D) + jnp.dot(mixed, out_weight, preferred_element_type=jnp.float32)
    stream_square = lax.optimization_barrier(jnp.mean(residual_sum * residual_sum, axis=-1, keepdims=True))
    normed = (residual_sum * lax.rsqrt(stream_square + 1e-06) * norm_gain).astype(jnp.bfloat16)
    token_groups = normed.reshape(SEQS, GROUPS, SUB, D).transpose(1, 0, 2, 3).reshape(GROUPS, TOK_DEV, D)
    residual_groups = residual_sum.reshape(SEQS, GROUPS, SUB, D).transpose(1, 0, 2, 3).reshape(GROUPS, TOK_DEV, D)
    picks = expert_ids.reshape(GROUPS, 2 * TOK_DEV)
    one_hot = (picks[:, :, None] == jnp.arange(EXPERTS, dtype=jnp.int32)[None, None, :]).astype(jnp.int32)
    ranking = lax.optimization_barrier(jnp.sum(jnp.cumsum(one_hot, axis=1) * one_hot, axis=2)) - 1
    slot_of = (picks * MOST + ranking).astype(jnp.int32)
    copies = jnp.repeat(token_groups, 2, axis=1)

    def place_group(slot_row, copy_rows):
        return jnp.zeros((EXPERTS * MOST, D), jnp.bfloat16).at[slot_row].set(copy_rows)
    dispatch = jax.vmap(place_group)(slot_of, copies)
    per_expert = dispatch.reshape(GROUPS, EXPERTS, MOST, D).transpose(1, 0, 2, 3).reshape(EXPERTS, GROUPS * MOST, D)

    def run_expert(inputs):
        slot_rows, gate_part, up_part, down_part = inputs
        summed = jnp.zeros((GROUPS * MOST, D), jnp.float32)
        for group_no in range(N_CTX):
            lower_edge = group_no * HID_DEV
            gate_val = jnp.dot(slot_rows, gate_part[:, lower_edge:lower_edge + HID_DEV], preferred_element_type=jnp.float32)
            up_val = jnp.dot(slot_rows, up_part[:, lower_edge:lower_edge + HID_DEV], preferred_element_type=jnp.float32)
            hidden = (jax.nn.silu(gate_val) * up_val).astype(jnp.bfloat16)
            partial_value = jnp.dot(hidden, down_part[lower_edge:lower_edge + HID_DEV], preferred_element_type=jnp.float32).astype(jnp.bfloat16)
            summed = summed + partial_value.astype(jnp.float32)
        return summed.astype(jnp.bfloat16)
    expert_out = lax.map(run_expert, (per_expert, w_gate, w_up, w_down))
    returned = expert_out.reshape(EXPERTS, GROUPS, MOST, D).transpose(1, 0, 2, 3).reshape(GROUPS, EXPERTS * MOST, D)
    picked = jnp.take_along_axis(returned, slot_of[:, :, None], axis=1).astype(jnp.float32)
    shares = expert_share.reshape(GROUPS, 2 * TOK_DEV, 1)
    expert_mix = lax.optimization_barrier(jnp.sum((picked * shares).reshape(GROUPS, TOK_DEV, 2, D), axis=2))
    result = (residual_groups + expert_mix).astype(jnp.bfloat16)
    return result.reshape(GROUPS, SEQS, SUB, D).transpose(1, 0, 2, 3).reshape(SEQS, SEQUENCE_LENGTH, D)
```

```python
import functools

import jax
import jax.numpy as jnp
from jax import lax
from jax.experimental import pallas as pl
from jax.experimental.pallas import tpu as pltpu
from jax.sharding import PartitionSpec as P

MIB = 1 << 20
BF = jnp.bfloat16
F32 = jnp.float32


def routes(count):
    bits = [1 << b for b in range(1, count.bit_length() - 1)]
    turn = len(bits) // 2
    return bits, bits[turn:] + bits[:turn]


def hop(count, step):
    both = routes(count)
    return [(i, i ^ both[i & 1][step]) for i in range(count)]


def hop_mask(count, step, side):
    both = routes(count)
    return jnp.where(side == 0, both[0][step], both[1][step])


def pair(count):
    return [(i, i ^ 1) for i in range(count)]


def held_by(count, who):
    held = [who]
    for step in range(len(routes(count)[0])):
        mask = hop_mask(count, step, who & 1)
        held = held + [h ^ mask for h in held]
    return held


def block_order(count, me):
    return held_by(count, me) + held_by(count, me ^ 1)


def send(x, perm):
    return lax.ppermute(x, "ctx", perm)


def joined(parts):
    return parts[0] if len(parts) == 1 else jnp.concatenate(parts, axis=0)


def spread(x, count):
    pieces = [x[None]]
    for step in range(len(routes(count)[0])):
        pieces.append(send(joined(pieces), hop(count, step)))
    pieces.append(send(joined(pieces), pair(count)))
    return pieces


def gathered_sum(near, far, count):
    total = near.astype(F32) + send(far, pair(count)).astype(F32)
    for step in reversed(range(len(routes(count)[0]))):
        half = total.shape[0] // 2
        other = send(total[half:].astype(BF), hop(count, step))
        total = total[:half] + other.astype(F32)
    return total[0]


def sum_over(x, count):
    for bit in range(count.bit_length() - 1):
        x = x + send(x, [(i, i ^ (1 << bit)) for i in range(count)])
    return x


def swap_blocks(x, count, me):
    got = [lax.dynamic_index_in_dim(x, me, 0, False)]
    for j in range(1, count):
        got.append(
            send(
                lax.dynamic_index_in_dim(x, me ^ j, 0, False),
                [(i, i ^ j) for i in range(count)],
            )
        )
    return got


def by_sender(got, count, me):
    stacked = jnp.stack(got)
    return jnp.stack(
        [lax.dynamic_index_in_dim(stacked, me ^ j, 0, False) for j in range(count)]
    )


def state_kernel(dim, k_ref, v_ref, cum_ref, out_ref):
    cum = cum_ref[...]
    fade = jnp.exp(cum[-1:, :] - cum)
    for h in range(cum.shape[1]):
        lanes = slice(h * dim, (h + 1) * dim)
        faded = (k_ref[0, :, lanes].astype(F32) * fade[:, h : h + 1]).astype(BF)
        out_ref[0, h] = lax.dot_general(
            faded, v_ref[0, :, lanes], (((0,), (0,)), ((), ())), preferred_element_type=F32
        ).astype(BF)


def local_states(keys, values, cum, first, seqs):
    _, block, width = keys.shape
    heads = cum.shape[1]
    dim = width // heads
    rows = pl.BlockSpec((1, block, width), lambda s: (s + first, 0, 0))
    return pl.pallas_call(
        functools.partial(state_kernel, dim),
        grid=(seqs,),
        in_specs=[rows, rows, pl.BlockSpec((block, heads), lambda s: (0, 0))],
        out_specs=pl.BlockSpec((1, heads, dim, dim), lambda s: (s, 0, 0, 0)),
        out_shape=jax.ShapeDtypeStruct((seqs, heads, dim, dim), BF),
        compiler_params=pltpu.CompilerParams(vmem_limit_bytes=16 * MIB),
        cost_estimate=pl.CostEstimate(
            flops=2 * seqs * block * width * dim,
            bytes_accessed=4 * seqs * block * width + 2 * seqs * width * dim,
            transcendentals=0,
        ),
    )(keys, values, cum)


def within_kernel(dim, q_ref, k_ref, v_ref, g_ref, cum_ref, cumt_ref, gain_ref, out_ref, act_ref):
    cum = cum_ref[...]
    block = cum.shape[0]
    causal = lax.broadcasted_iota(jnp.int32, (block, block), 0) >= lax.broadcasted_iota(
        jnp.int32, (block, block), 1
    )
    for h in range(cum.shape[1]):
        lanes = slice(h * dim, (h + 1) * dim)
        scores = lax.dot_general(
            q_ref[0, :, lanes],
            k_ref[0, :, lanes],
            (((1,), (1,)), ((), ())),
            preferred_element_type=F32,
        )
        gap = jnp.where(causal, cum[:, h : h + 1] - cumt_ref[h : h + 1, :], -1e30)
        weights = (scores * jnp.exp(gap)).astype(BF)
        out_ref[0, :, lanes] = jnp.dot(weights, v_ref[0, :, lanes], preferred_element_type=F32)
    act_ref[0] = gain_ref[...] * jax.nn.sigmoid(g_ref[0].astype(F32))


def within_block(queries, keys, values, gate, cum, head_gain):
    seqs, block, width = keys.shape
    heads = cum.shape[1]
    dim = width // heads
    rows = pl.BlockSpec((1, block, width), lambda s: (s, 0, 0))
    shape = jax.ShapeDtypeStruct((seqs, block, width), F32)
    return pl.pallas_call(
        functools.partial(within_kernel, dim),
        grid=(seqs,),
        in_specs=[
            rows,
            rows,
            rows,
            rows,
            pl.BlockSpec((block, heads), lambda s: (0, 0)),
            pl.BlockSpec((heads, block), lambda s: (0, 0)),
            pl.BlockSpec((1, width), lambda s: (0, 0)),
        ],
        out_specs=[rows, rows],
        out_shape=[shape, shape],
        compiler_params=pltpu.CompilerParams(vmem_limit_bytes=24 * MIB),
        cost_estimate=pl.CostEstimate(
            flops=4 * seqs * block * block * width,
            bytes_accessed=16 * seqs * block * width,
            transcendentals=seqs * block * width,
        ),
    )(queries, keys, values, gate, cum, cum.T, head_gain[None])


def mixed_kernel(dim, sub, q_ref, state_ref, within_ref, act_ref, cum_ref, out_ref):
    scale = jnp.exp(cum_ref[...])
    for h in range(scale.shape[1]):
        lanes = slice(h * dim, (h + 1) * dim)
        carried = jnp.dot(q_ref[0, :, lanes], state_ref[0, h], preferred_element_type=F32)
        attended = within_ref[0, :, lanes] + carried * scale[:, h : h + 1]
        square = jnp.mean(attended * attended, axis=1, keepdims=True)
        mixed = (attended * lax.rsqrt(square + 1e-06) * act_ref[0, :, lanes]).astype(BF)
        for d in range(out_ref.shape[0]):
            out_ref[d, 0, :, lanes] = mixed[d * sub : (d + 1) * sub]


def mixed_rows(queries, states, within, act, cum, first, sub):
    seqs, heads, dim, _ = states.shape
    block, width = queries.shape[1:]
    parts = block // sub
    rows = pl.BlockSpec((1, block, width), lambda s: (s + first, 0, 0))
    return pl.pallas_call(
        functools.partial(mixed_kernel, dim, sub),
        grid=(seqs,),
        in_specs=[
            rows,
            pl.BlockSpec((1, heads, dim, dim), lambda s: (s, 0, 0, 0)),
            rows,
            rows,
            pl.BlockSpec((block, heads), lambda s: (0, 0)),
        ],
        out_specs=pl.BlockSpec((parts, 1, sub, width), lambda s: (0, s, 0, 0)),
        out_shape=jax.ShapeDtypeStruct((parts, seqs, sub, width), BF),
        compiler_params=pltpu.CompilerParams(vmem_limit_bytes=16 * MIB),
        cost_estimate=pl.CostEstimate(
            flops=2 * seqs * block * width * dim,
            bytes_accessed=12 * seqs * block * width + 2 * seqs * width * dim,
            transcendentals=0,
        ),
    )(queries, states, within, act, cum)


def project_kernel(sizes, order_ref, *refs):
    pieces, w_ref, out_ref = refs[:-2], refs[-2], refs[-1]
    parts, _, rows, _ = out_ref.shape
    at = 0
    for ref, size in zip(pieces, sizes):
        for i in range(size):
            product = jnp.dot(ref[i], w_ref[...], preferred_element_type=F32).astype(BF)
            for d in range(parts):
                out_ref[d, order_ref[at]] = product[d * rows : (d + 1) * rows]
            at += 1


def project(pieces, weight, order, parts):
    count = sum(p.shape[0] for p in pieces)
    rows, depth = pieces[0].shape[1:]
    cols = weight.shape[1]
    whole = pl.BlockSpec(memory_space=pltpu.VMEM)
    return pl.pallas_call(
        functools.partial(project_kernel, [p.shape[0] for p in pieces]),
        in_specs=[pl.BlockSpec(memory_space=pltpu.SMEM)] + [whole] * (len(pieces) + 1),
        out_specs=whole,
        out_shape=jax.ShapeDtypeStruct((parts, count, rows // parts, cols), BF),
        compiler_params=pltpu.CompilerParams(vmem_limit_bytes=20 * MIB),
        cost_estimate=pl.CostEstimate(
            flops=2 * count * rows * depth * cols,
            bytes_accessed=2 * (count * rows * (depth + cols) + depth * cols),
            transcendentals=0,
        ),
    )(order, *pieces, weight)


def expert_kernel(sizes, order_ref, *refs):
    count = sum(sizes)
    half = count // 2
    pieces = refs[: len(sizes)]
    scale_ref, gate_ref, up_ref, down_ref, near_ref, far_ref, g_acc, u_acc, hidden = refs[
        len(sizes) :
    ]
    i = pl.program_id(0)

    @pl.when(i == 0)
    def _():
        g_acc[...] = jnp.dot(pieces[0][0], gate_ref[...], preferred_element_type=F32)
        u_acc[...] = jnp.dot(pieces[0][0], up_ref[...], preferred_element_type=F32)

    start = 0
    for ref, size in zip(pieces, sizes):
        if start > 0:

            @pl.when((i >= start) & (i < start + size))
            def _(ref=ref):
                g_acc[...] += jnp.dot(ref[0], gate_ref[...], preferred_element_type=F32)
                u_acc[...] += jnp.dot(ref[0], up_ref[...], preferred_element_type=F32)

        start += size

    @pl.when(i == count - 1)
    def _():
        scale = scale_ref[...]
        g = g_acc[...] * scale
        hidden[...] = (g / (1.0 + jnp.exp(-g)) * (u_acc[...] * scale)).astype(BF)

    @pl.when((i >= count) & (i < count + half))
    def _():
        far_ref[0] = jnp.dot(hidden[...], down_ref[...], preferred_element_type=F32).astype(BF)

    @pl.when(i >= count + half)
    def _():
        near_ref[0] = jnp.dot(hidden[...], down_ref[...], preferred_element_type=F32).astype(BF)


def expert(pieces, scale, w_gate, w_up, w_down, order):
    sizes = [p.shape[0] for p in pieces]
    count = sum(sizes)
    half = count // 2
    rows, cols = pieces[0].shape[1:]
    depth, hid = w_gate.shape

    def up_map(i, order):
        return (order[jnp.minimum(i, count - 1)], 0)

    def down_map(i, order):
        j = jnp.maximum(i - count, 0)
        return (0, order[jnp.where(j < half, j + half, j - half)])

    specs = []
    start = 0
    for size in sizes:
        specs.append(
            pl.BlockSpec(
                (1, rows, cols),
                lambda i, order, start=start, size=size: (
                    jnp.clip(i - start, 0, size - 1),
                    0,
                    0,
                ),
            )
        )
        start += size
    out = jax.ShapeDtypeStruct((half, rows, cols), BF)
    return pl.pallas_call(
        functools.partial(expert_kernel, sizes),
        grid_spec=pltpu.PrefetchScalarGridSpec(
            num_scalar_prefetch=1,
            grid=(2 * count,),
            in_specs=specs
            + [
                pl.BlockSpec((rows, 1), lambda i, order: (0, 0)),
                pl.BlockSpec((cols, hid), up_map),
                pl.BlockSpec((cols, hid), up_map),
                pl.BlockSpec((hid, cols), down_map),
            ],
            out_specs=[
                pl.BlockSpec(
                    (1, rows, cols),
                    lambda i, order: (jnp.clip(i - count - half, 0, half - 1), 0, 0),
                ),
                pl.BlockSpec(
                    (1, rows, cols), lambda i, order: (jnp.clip(i - count, 0, half - 1), 0, 0)
                ),
            ],
            scratch_shapes=[
                pltpu.VMEM((rows, hid), F32),
                pltpu.VMEM((rows, hid), F32),
                pltpu.VMEM((rows, hid), BF),
            ],
        ),
        out_shape=[out, out],
        compiler_params=pltpu.CompilerParams(vmem_limit_bytes=32 * MIB),
        cost_estimate=pl.CostEstimate(
            flops=6 * rows * depth * hid,
            bytes_accessed=6 * depth * hid + 4 * rows * depth,
            transcendentals=rows * hid,
        ),
    )(order, *pieces, scale, w_gate, w_up, w_down)


def body(
    queries,
    keys,
    values,
    decay_log,
    out_gate,
    head_gain,
    out_weight,
    stream,
    norm_gain,
    expert_ids,
    expert_share,
    w_gate,
    w_up,
    w_down,
):
    count = lax.axis_size("ctx")
    parts = lax.axis_size("exp")
    me = lax.axis_index("ctx")
    mine = lax.axis_index("exp")
    side = me & 1
    seqs, block, width = queries.shape
    heads = decay_log.shape[1]
    sub, model = stream.shape[1:]
    tokens = seqs * sub
    cols = model // count
    order = block_order(count, me)
    order_array = jnp.stack(order).astype(jnp.int32)

    cum = jnp.cumsum(decay_log, axis=0)
    small = jnp.concatenate(
        [
            expert_ids.reshape(2 * tokens).astype(F32),
            expert_share.reshape(2 * tokens),
            cum[-1],
        ]
    )
    width_small = small.shape[0]
    small = jnp.pad(small, (0, -width_small % 128)).reshape(-1, 128)
    facts = joined(spread(small, count)).reshape(count, -1)
    place = order_array[None, :] == jnp.arange(count, dtype=jnp.int32)[:, None]
    facts = jnp.sum(jnp.where(place[:, :, None], facts[None], 0.0), axis=1)
    ids = facts[:, : 2 * tokens].astype(jnp.int32)
    shares = facts[:, 2 * tokens : 4 * tokens]
    ends = facts[:, 4 * tokens : 4 * tokens + heads]

    stream_cols = stream.reshape(tokens, count, cols).transpose(1, 0, 2)
    stream_got = swap_blocks(stream_cols, count, me)

    block_no = jnp.arange(count)

    def faded(source, target):
        between = (block_no >= 2 * (source // 2 + 1)) & (block_no < 2 * (target // 2))
        power = jnp.sum(jnp.where(between[:, None], ends, 0.0), axis=0)
        return jnp.where(source // 2 < target // 2, jnp.exp(power), 0.0)

    def at_heads(row):
        return row[None, :, None, None]

    half_heads = heads // 2

    def side_half(x, axis):
        return lax.dynamic_slice_in_dim(x, side * half_heads, half_heads, axis)

    fade_own = jnp.exp(lax.dynamic_index_in_dim(ends, me, 0, False))
    fade_other = jnp.exp(lax.dynamic_index_in_dim(ends, me ^ 1, 0, False))
    steps = len(routes(count)[0])

    def arriving(own, other):
        fade_late = jnp.where(side == 0, fade_other, fade_own)
        own_half, other_half = side_half(own, 1).astype(F32), side_half(other, 1).astype(F32)
        early = jnp.where(side == 0, own_half, other_half)
        late = jnp.where(side == 0, other_half, own_half)
        chip = (at_heads(side_half(fade_late, 0)) * early + late).astype(BF)
        held, names = [chip], [me]
        for step in range(steps - 1):
            stacked = jnp.stack(held)
            got = send(stacked, hop(count, step))
            mask = hop_mask(count, step, side)
            held = held + [got[i] for i in range(len(held))]
            names = names + [name ^ mask for name in names]

        def towards(target):
            return sum(
                at_heads(side_half(faded(name, target), 0)) * state.astype(F32)
                for name, state in zip(names, held)
            )

        entering = towards(me)
        if steps:
            there = me ^ hop_mask(count, steps - 1, side)
            entering = entering + send(towards(there).astype(BF), hop(count, steps - 1)).astype(F32)
        entering = entering.astype(BF)
        entering_other = send(entering, pair(count))
        low = jnp.where(side == 0, entering, entering_other)
        high = jnp.where(side == 0, entering_other, entering)
        entering = jnp.concatenate([low, high], axis=1).astype(F32)
        second = at_heads(fade_other) * entering + other.astype(F32)
        return jnp.where(side == 0, entering, second).astype(BF)

    halves = 2
    each = seqs // halves
    own_states = [local_states(keys, values, cum, h * each, each) for h in range(halves)]
    other_states = [send(own, pair(count)) for own in own_states]
    within, act = within_block(queries, keys, values, out_gate, cum, head_gain)
    projected = []
    for h in range(halves):
        states = arriving(own_states[h], other_states[h])
        mixed = mixed_rows(queries, states, within, act, cum, h * each, sub)
        pieces = spread(mixed.reshape(parts * each * sub, width), count)
        partial = project(pieces, out_weight, order_array, parts)

        def part(index):
            return lax.dynamic_index_in_dim(
                partial, jnp.clip(index, 0, parts - 1), 0, False
            ).astype(F32)

        total = part(mine)
        for way in (1, -1):
            passed = None
            for t in range(parts - 1):
                if way == 1:
                    perm = [(i, i + 1) for i in range(parts - 1) if i <= t]
                else:
                    perm = [(i, i - 1) for i in range(1, parts) if parts - 1 - i <= t]
                running = part(mine + way * (parts - 1 - t))
                if passed is not None:
                    running = running + passed.astype(F32)
                passed = lax.ppermute(running.astype(BF), "exp", perm)
            if passed is not None:
                total = total + passed.astype(F32)
        projected.append(total)
    stream_all = by_sender(stream_got, count, me)
    residual = stream_all.astype(F32) + jnp.concatenate(projected, axis=1)
    residual = residual.reshape(count * tokens, cols)

    square = sum_over(jnp.sum(residual * residual, axis=1), count)
    scale = lax.rsqrt(square / model + 1e-06)
    gain = lax.dynamic_slice_in_dim(norm_gain, me * cols, cols, 0)
    rows_in = (residual * gain).astype(BF)

    expert_local = w_gate.shape[0]
    experts = expert_local * parts
    capacity = max(2, (2 * tokens + experts - 1) // experts + 1)
    one_hot = ids[:, :, None] == jnp.arange(experts, dtype=jnp.int32)
    earlier = jnp.arange(2 * tokens)[:, None] > jnp.arange(2 * tokens)[None, :]
    ahead = jnp.einsum(
        "tu,gue->gte", earlier.astype(BF), one_hot.astype(BF), preferred_element_type=F32
    )
    ranking = jnp.sum(jnp.where(one_hot, ahead, 0.0), axis=2).astype(jnp.int32)
    slots = capacity * count
    turned = (ids - mine + experts) % experts
    slot_of = (turned * count + jnp.arange(count, dtype=jnp.int32)[:, None]) * capacity + ranking
    slot_of = slot_of.reshape(count * tokens, 2)
    share_of = shares.reshape(count * tokens, 2)
    returned = []
    for turn in range(parts):
        numbers = turn * slots + jnp.arange(slots, dtype=jnp.int32)
        hit = [slot_of[:, k][None, :] == numbers[:, None] for k in range(2)]
        placing = hit[0] | hit[1]
        dispatch = jnp.dot(placing.astype(BF), rows_in, preferred_element_type=F32).astype(BF)
        slot_scale = jnp.sum(jnp.where(placing, scale[None, :], 0.0), axis=1)
        forth = [(i, (i + turn) % parts) for i in range(parts)]
        back = [(j, i) for i, j in forth]
        if turn:
            dispatch = lax.ppermute(dispatch, "exp", forth)
            slot_scale = lax.ppermute(slot_scale, "exp", forth)
        pieces = spread(dispatch, count)
        near, far = expert(
            pieces, slot_scale[:, None], w_gate[0], w_up[0], w_down[0], order_array
        )
        done = gathered_sum(near, far, count).astype(BF)
        if turn:
            done = lax.ppermute(done, "exp", back)
        returned.append(done)
    result = residual
    for turn in range(parts):
        numbers = turn * slots + jnp.arange(slots, dtype=jnp.int32)
        weighting = sum(
            jnp.where(slot_of[:, k][:, None] == numbers[None, :], share_of[:, k][:, None], 0.0)
            for k in range(2)
        )
        high = weighting.astype(BF)
        low = (weighting - high.astype(F32)).astype(BF)
        result = result + jnp.dot(high, returned[turn], preferred_element_type=F32)
        result = result + jnp.dot(low, returned[turn], preferred_element_type=F32)
    result = result.astype(BF).reshape(count, tokens, cols)
    result = by_sender(swap_blocks(result, count, me), count, me)
    return result.transpose(1, 0, 2).reshape(seqs, sub, model)


def solution(mesh):
    return jax.shard_map(
        body,
        mesh=mesh,
        in_specs=(
            P(None, "ctx", "exp"),
            P(None, "ctx", "exp"),
            P(None, "ctx", "exp"),
            P("ctx", "exp"),
            P(None, "ctx", "exp"),
            P("exp"),
            P("exp", "ctx"),
            P(None, ("ctx", "exp"), None),
            P(),
            P(("ctx", "exp"), None, None),
            P(("ctx", "exp"), None, None),
            P("exp", None, "ctx"),
            P("exp", None, "ctx"),
            P("exp", "ctx", None),
        ),
        out_specs=P(None, ("ctx", "exp"), None),
        check_vma=False,
    )
```

```python
import functools

import jax
import jax.numpy as jnp
from jax import lax
from jax.experimental import pallas as pl
from jax.experimental.pallas import tpu as pltpu
from jax.sharding import PartitionSpec as P

MIB = 1 << 20
BF = jnp.bfloat16
F32 = jnp.float32


def routes(count):
    bits = [1 << b for b in range(1, count.bit_length() - 1)]
    turn = len(bits) // 2
    return bits, bits[turn:] + bits[:turn]


def hop(count, step):
    both = routes(count)
    return [(i, i ^ both[i & 1][step]) for i in range(count)]


def hop_mask(count, step, side):
    both = routes(count)
    return jnp.where(side == 0, both[0][step], both[1][step])


def pair(count):
    return [(i, i ^ 1) for i in range(count)]


def held_by(count, who):
    held = [who]
    for step in range(len(routes(count)[0])):
        mask = hop_mask(count, step, who & 1)
        held = held + [h ^ mask for h in held]
    return held


def block_order(count, me):
    return held_by(count, me) + held_by(count, me ^ 1)


def send(x, perm):
    return lax.ppermute(x, "ctx", perm)


def after(x, *others):
    return lax.optimization_barrier((x, *others))[0]


def joined(parts):
    return parts[0] if len(parts) == 1 else jnp.concatenate(parts, axis=0)


def spread(x, count, gates=()):
    pieces = [x[None]]
    for step in range(len(routes(count)[0])):
        block = joined(pieces)
        if step < len(gates):
            block = after(block, *gates[step])
        pieces.append(send(block, hop(count, step)))
    block = tuple(pieces)
    if len(gates) > len(routes(count)[0]):
        block = after(block, *gates[-1])
    return pieces + [send(x, pair(count)) for x in block]


def pair_sum(near, far, count):
    return (near.astype(F32) + send(far, pair(count)).astype(F32)).astype(BF)


def gathered_sum(total, count, gates=()):
    got = []
    for at, step in enumerate(reversed(range(len(routes(count)[0])))):
        half = total.shape[0] // 2
        leaving = total[half:]
        if at < len(gates):
            leaving = after(leaving, *gates[at])
        other = send(leaving, hop(count, step))
        got.append(other)
        total = (total[:half].astype(F32) + other.astype(F32)).astype(BF)
    return total[0], got


def sum_over(x, count):
    for bit in range(count.bit_length() - 1):
        x = x + send(x, [(i, i ^ (1 << bit)) for i in range(count)])
    return x


def swap_blocks(blocks, count):
    got = [blocks[0]]
    for j in range(1, count):
        got.append(send(blocks[j], [(i, i ^ j) for i in range(count)]))
    return got


def cut_kernel(mates_ref, x_ref, *outs):
    cols = outs[0].shape[1]
    for j, out in enumerate(outs):
        out[...] = x_ref[:, pl.ds(pl.multiple_of(mates_ref[j] * cols, cols), cols)]


def cut_columns(x, mates):
    rows, width = x.shape
    count = mates.shape[0]
    whole = pl.BlockSpec(memory_space=pltpu.VMEM)
    shape = jax.ShapeDtypeStruct((rows, width // count), x.dtype)
    return pl.pallas_call(
        cut_kernel,
        in_specs=[pl.BlockSpec(memory_space=pltpu.SMEM), whole],
        out_specs=[whole] * count,
        out_shape=[shape] * count,
    )(mates, x)


def lay_kernel(mates_ref, *refs):
    *blocks, out_ref = refs
    cols = blocks[0].shape[1]
    for j, ref in enumerate(blocks):
        out_ref[:, pl.ds(pl.multiple_of(mates_ref[j] * cols, cols), cols)] = ref[...]


def lay_columns(blocks, mates):
    rows, cols = blocks[0].shape
    whole = pl.BlockSpec(memory_space=pltpu.VMEM)
    return pl.pallas_call(
        lay_kernel,
        in_specs=[pl.BlockSpec(memory_space=pltpu.SMEM)] + [whole] * len(blocks),
        out_specs=whole,
        out_shape=jax.ShapeDtypeStruct((rows, cols * len(blocks)), blocks[0].dtype),
    )(mates, *blocks)


def state_kernel(dim, place_ref, k_ref, v_ref, cum_ref, out_ref):
    cum = cum_ref[...]
    fade = jnp.exp(cum[-1:, :] - cum)
    for h in range(cum.shape[1]):
        lanes = slice(h * dim, (h + 1) * dim)
        faded = (k_ref[0, :, lanes].astype(F32) * fade[:, h : h + 1]).astype(BF)
        out_ref[0, h] = lax.dot_general(
            faded, v_ref[0, :, lanes], (((0,), (0,)), ((), ())), preferred_element_type=F32
        ).astype(BF)


def local_states(keys, values, cum, place):
    seqs, block, width = keys.shape
    heads = cum.shape[1]
    dim = width // 2 // heads
    rows = pl.BlockSpec((1, block, width // 2), lambda s, place: (s, 0, place[0]))
    return pl.pallas_call(
        functools.partial(state_kernel, dim),
        grid_spec=pltpu.PrefetchScalarGridSpec(
            num_scalar_prefetch=1,
            grid=(seqs,),
            in_specs=[rows, rows, pl.BlockSpec((block, heads), lambda s, place: (0, 0))],
            out_specs=pl.BlockSpec((1, heads, dim, dim), lambda s, place: (s, 0, 0, 0)),
        ),
        out_shape=jax.ShapeDtypeStruct((seqs, heads, dim, dim), BF),
        compiler_params=pltpu.CompilerParams(vmem_limit_bytes=60 * MIB),
        cost_estimate=pl.CostEstimate(
            flops=2000000000, bytes_accessed=2 * seqs * width * (block + dim), transcendentals=0
        ),
    )(place.reshape(1).astype(jnp.int32), keys, values, cum)


def within_kernel(dim, q_ref, k_ref, v_ref, g_ref, cum_ref, cumt_ref, gain_ref, out_ref, act_ref):
    cum = cum_ref[...]
    block = cum.shape[0]
    causal = lax.broadcasted_iota(jnp.int32, (block, block), 0) >= lax.broadcasted_iota(
        jnp.int32, (block, block), 1
    )
    for h in range(cum.shape[1]):
        lanes = slice(h * dim, (h + 1) * dim)
        scores = lax.dot_general(
            q_ref[0, :, lanes],
            k_ref[0, :, lanes],
            (((1,), (1,)), ((), ())),
            preferred_element_type=F32,
        )
        gap = jnp.where(causal, cum[:, h : h + 1] - cumt_ref[h : h + 1, :], -1e30)
        weights = (scores * jnp.exp(gap)).astype(BF)
        out_ref[0, :, lanes] = jnp.dot(weights, v_ref[0, :, lanes], preferred_element_type=F32)
    act_ref[0] = gain_ref[...] * jax.nn.sigmoid(g_ref[0].astype(F32))


def within_block(queries, keys, values, gate, cum, head_gain):
    seqs, block, width = keys.shape
    heads = cum.shape[1]
    dim = width // heads
    rows = pl.BlockSpec((1, block, width), lambda s: (s, 0, 0))
    shape = jax.ShapeDtypeStruct((seqs, block, width), F32)
    return pl.pallas_call(
        functools.partial(within_kernel, dim),
        grid=(seqs,),
        in_specs=[
            rows,
            rows,
            rows,
            rows,
            pl.BlockSpec((block, heads), lambda s: (0, 0)),
            pl.BlockSpec((heads, block), lambda s: (0, 0)),
            pl.BlockSpec((1, width), lambda s: (0, 0)),
        ],
        out_specs=[rows, rows],
        out_shape=[shape, shape],
        compiler_params=pltpu.CompilerParams(vmem_limit_bytes=60 * MIB),
        cost_estimate=pl.CostEstimate(
            flops=60 * seqs * block * block * width,
            bytes_accessed=16 * seqs * block * width,
            transcendentals=seqs * block * width,
        ),
    )(queries, keys, values, gate, cum, cum.T, head_gain[None])


def combine_kernel(weight_ref, *refs):
    *states, out_ref = refs
    for h in range(out_ref.shape[1]):
        out_ref[0, h] = sum(
            weight_ref[i, h] * ref[0, h].astype(F32) for i, ref in enumerate(states)
        ).astype(BF)


def combine(states, weights):
    seqs, heads, dim, _ = states[0].shape
    block = pl.BlockSpec((1, heads, dim, dim), lambda s: (s, 0, 0, 0))
    return pl.pallas_call(
        combine_kernel,
        grid=(seqs,),
        in_specs=[pl.BlockSpec(memory_space=pltpu.SMEM)] + [block] * len(states),
        out_specs=block,
        out_shape=jax.ShapeDtypeStruct(states[0].shape, BF),
        compiler_params=pltpu.CompilerParams(vmem_limit_bytes=16 * MIB),
    )(weights, *states)


def mixed_kernel(
    dim, sub, side_ref, weight_ref, q_ref, own_ref, got_ref, pair_own_ref, pair_got_ref,
    within_ref, act_ref, cum_ref, out_ref,
):
    scale = jnp.exp(cum_ref[...])
    heads = scale.shape[1]
    half = heads // 2
    for h in range(heads):
        lanes = slice(h * dim, (h + 1) * dim)
        here = side_ref[0] == h // half
        entering = jnp.where(here, own_ref[0, h % half], got_ref[0, h % half]).astype(F32)
        paired = jnp.where(here, pair_own_ref[0, h % half], pair_got_ref[0, h % half]).astype(F32)
        state = (weight_ref[0, h] * entering + weight_ref[1, h] * paired).astype(BF)
        carried = jnp.dot(q_ref[0, :, lanes], state, preferred_element_type=F32)
        attended = within_ref[0, :, lanes] + carried * scale[:, h : h + 1]
        square = jnp.mean(attended * attended, axis=1, keepdims=True)
        mixed = (attended * lax.rsqrt(square + 1e-06) * act_ref[0, :, lanes]).astype(BF)
        for d in range(out_ref.shape[0]):
            out_ref[d, 0, :, lanes] = mixed[d * sub : (d + 1) * sub]


def mixed_rows(queries, states, weights, side, within, act, cum, sub, first, seqs):
    _, block, width = queries.shape
    heads = cum.shape[1]
    dim = width // heads
    parts = block // sub
    rows = pl.BlockSpec((1, block, width), lambda s, side: (s + first, 0, 0))
    halved = pl.BlockSpec((1, heads // 2, dim, dim), lambda s, side: (s + first, 0, 0, 0))
    return pl.pallas_call(
        functools.partial(mixed_kernel, dim, sub),
        grid_spec=pltpu.PrefetchScalarGridSpec(
            num_scalar_prefetch=1,
            grid=(seqs,),
            in_specs=[pl.BlockSpec(memory_space=pltpu.SMEM), rows]
            + [halved] * 4
            + [rows, rows, pl.BlockSpec((block, heads), lambda s, side: (0, 0))],
            out_specs=pl.BlockSpec((parts, 1, sub, width), lambda s, side: (0, s, 0, 0)),
        ),
        out_shape=jax.ShapeDtypeStruct((parts, seqs, sub, width), BF),
        compiler_params=pltpu.CompilerParams(vmem_limit_bytes=60 * MIB),
        cost_estimate=pl.CostEstimate(
            flops=6000000000, bytes_accessed=14 * seqs * block * width, transcendentals=0
        ),
    )(side.reshape(1).astype(jnp.int32), weights, queries, *states, within, act, cum)


def project_kernel(sizes, order_ref, *refs):
    *pieces, w_ref, out_ref = refs
    parts, _, rows, _ = out_ref.shape
    at = 0
    for ref, size in zip(pieces, sizes):
        for i in range(size):
            product = jnp.dot(ref[i], w_ref[...], preferred_element_type=F32).astype(BF)
            for d in range(parts):
                out_ref[d, order_ref[at]] = product[d * rows : (d + 1) * rows]
            at += 1


def project(pieces, weight, order, parts):
    count = sum(p.shape[0] for p in pieces)
    rows, depth = pieces[0].shape[1:]
    cols = weight.shape[1]
    whole = pl.BlockSpec(memory_space=pltpu.VMEM)
    return pl.pallas_call(
        functools.partial(project_kernel, [p.shape[0] for p in pieces]),
        in_specs=[pl.BlockSpec(memory_space=pltpu.SMEM)] + [whole] * (len(pieces) + 1),
        out_specs=whole,
        out_shape=jax.ShapeDtypeStruct((parts, count, rows // parts, cols), BF),
        compiler_params=pltpu.CompilerParams(vmem_limit_bytes=20 * MIB),
        cost_estimate=pl.CostEstimate(
            flops=4 * count * rows * depth * cols,
            bytes_accessed=2 * (count * rows * (depth + cols) + depth * cols),
            transcendentals=0,
        ),
    )(order, *pieces, weight)


def residual_kernel(count, mates_ref, *refs):
    stream, sums = refs[:count], refs[count:-2]
    out_ref, square_ref = refs[-2:]
    rows = out_ref.shape[1] // len(sums)
    for j in range(count):
        out_ref[mates_ref[j]] = stream[j][...].astype(F32)
    for b in range(count):
        for h, ref in enumerate(sums):
            at = slice(h * rows, (h + 1) * rows)
            total = out_ref[b, at] + ref[b].astype(F32)
            out_ref[b, at] = total
            square_ref[b, at] = jnp.sum(total * total, axis=1, keepdims=True)


def residual_sums(mates, stream, sums):
    count = len(stream)
    rows, cols = stream[0].shape
    whole = pl.BlockSpec(memory_space=pltpu.VMEM)
    return pl.pallas_call(
        functools.partial(residual_kernel, count),
        in_specs=[pl.BlockSpec(memory_space=pltpu.SMEM)] + [whole] * (count + len(sums)),
        out_specs=[whole] * 2,
        out_shape=[
            jax.ShapeDtypeStruct((count, rows, cols), F32),
            jax.ShapeDtypeStruct((count, rows, 1), F32),
        ],
        compiler_params=pltpu.CompilerParams(vmem_limit_bytes=32 * MIB),
    )(mates, *stream, *sums)


def hidden_kernel(sizes, groups, order_ref, *refs):
    steps = sum(sizes)
    each = len(sizes)
    pieces = [refs[g * each : (g + 1) * each] for g in range(groups)]
    refs = refs[groups * each :]
    (gate_ref, up_ref), outs = refs[:2], refs[2:]
    outs, g_acc, u_acc = outs[:groups], outs[-2], outs[-1]
    i = pl.program_id(0)

    start = 0
    for p, size in enumerate(sizes):

        @pl.when((i >= start) & (i < start + size))
        def _(p=p, start=start):
            for g in range(groups):
                rows = pieces[g][p][0]
                gate = jnp.dot(rows, gate_ref[...], preferred_element_type=F32)
                up = jnp.dot(rows, up_ref[...], preferred_element_type=F32)
                if start == 0:
                    g_acc[g] = gate
                    u_acc[g] = up
                else:
                    g_acc[g] += gate
                    u_acc[g] += up

        start += size

    @pl.when(i == steps - 1)
    def _():
        for g in range(groups):
            v = g_acc[g]
            outs[g][...] = (v / (1.0 + jnp.exp(-v)) * u_acc[g]).astype(BF)


def hidden_units(groups, w_gate, w_up, order):
    sizes = [p.shape[0] for p in groups[0]]
    rows, cols = groups[0][0].shape[1:]
    depth, hid = w_gate.shape
    many = len(groups)
    specs = []
    start = 0
    for size in sizes:
        specs.append(
            pl.BlockSpec(
                (1, rows, cols),
                lambda i, order, start=start, size=size: (jnp.clip(i - start, 0, size - 1), 0, 0),
            )
        )
        start += size
    up_spec = pl.BlockSpec((cols, hid), lambda i, order: (order[i], 0))
    return pl.pallas_call(
        functools.partial(hidden_kernel, sizes, many),
        grid_spec=pltpu.PrefetchScalarGridSpec(
            num_scalar_prefetch=1,
            grid=(sum(sizes),),
            in_specs=specs * many
            + [up_spec, up_spec],
            out_specs=[pl.BlockSpec((rows, hid), lambda i, order: (0, 0))] * many,
            scratch_shapes=[pltpu.VMEM((many, rows, hid), F32)] * 2,
        ),
        out_shape=[jax.ShapeDtypeStruct((rows, hid), BF)] * many,
        compiler_params=pltpu.CompilerParams(vmem_limit_bytes=60 * MIB),
        cost_estimate=pl.CostEstimate(
            flops=8 * many * rows * depth * hid,
            bytes_accessed=4 * depth * hid + 2 * many * rows * depth,
            transcendentals=many * rows * hid,
        ),
    )(order, *[p for pieces in groups for p in pieces], w_gate, w_up)


def down_kernel(groups, order_ref, *refs):
    hidden, weight, outs = refs[:groups], refs[groups], refs[groups + 1 :]
    for g in range(groups):
        outs[g][0] = jnp.dot(hidden[g][...], weight[...], preferred_element_type=F32).astype(BF)


def down_blocks(hidden, w_down, order):
    many = len(hidden)
    rows, hid = hidden[0].shape
    blocks, model = order.shape[0], w_down.shape[1]
    cols = model // lax.axis_size("ctx")

    return pl.pallas_call(
        functools.partial(down_kernel, many),
        grid_spec=pltpu.PrefetchScalarGridSpec(
            num_scalar_prefetch=1,
            grid=(blocks,),
            in_specs=[pl.BlockSpec((rows, hid), lambda i, order: (0, 0))] * many
            + [pl.BlockSpec((hid, cols), lambda i, order: (0, order[i]))],
            out_specs=[pl.BlockSpec((1, rows, cols), lambda i, order: (i, 0, 0))] * many,
        ),
        out_shape=[jax.ShapeDtypeStruct((blocks, rows, cols), BF)] * many,
        compiler_params=pltpu.CompilerParams(vmem_limit_bytes=60 * MIB),
        cost_estimate=pl.CostEstimate(
            flops=4 * many * rows * cols * blocks * hid,
            bytes_accessed=2 * cols * blocks * hid + 2 * many * rows * cols * blocks,
            transcendentals=0,
        ),
    )(order, *hidden, w_down)


def body(
    queries,
    keys,
    values,
    decay_log,
    out_gate,
    head_gain,
    out_weight,
    stream,
    norm_gain,
    expert_ids,
    expert_share,
    w_gate,
    w_up,
    w_down,
):
    count = lax.axis_size("ctx")
    parts = lax.axis_size("exp")
    me = lax.axis_index("ctx")
    mine = lax.axis_index("exp")
    side = me & 1
    seqs, block, width = queries.shape
    heads = decay_log.shape[1]
    sub, model = stream.shape[1:]
    tokens = seqs * sub
    cols = model // count
    order = block_order(count, me)
    order_array = jnp.stack(order).astype(jnp.int32)

    cum = jnp.cumsum(decay_log, axis=0)
    small = jnp.concatenate(
        [
            expert_ids.reshape(2 * tokens).astype(F32),
            expert_share.reshape(2 * tokens),
            cum[-1],
        ]
    )
    width_small = small.shape[0]
    small = jnp.pad(small, (0, -width_small % 128)).reshape(-1, 128)
    facts = joined(spread(small, count)).reshape(count, -1)
    steps = len(routes(count)[0])
    place = order_array[None, :] == jnp.arange(count, dtype=jnp.int32)[:, None]
    facts = jnp.sum(jnp.where(place[:, :, None], facts[None], 0.0), axis=1)
    ids = facts[:, : 2 * tokens].astype(jnp.int32)
    shares = facts[:, 2 * tokens : 4 * tokens]
    ends = facts[:, 4 * tokens : 4 * tokens + heads]

    mates = (me ^ jnp.arange(count, dtype=jnp.int32)).astype(jnp.int32)

    block_no = jnp.arange(count)

    def faded(source, target):
        between = (block_no >= 2 * (source // 2 + 1)) & (block_no < 2 * (target // 2))
        power = jnp.sum(jnp.where(between[:, None], ends, 0.0), axis=0)
        return jnp.where(source // 2 < target // 2, jnp.exp(power), 0.0)

    half_heads = heads // 2

    def side_half(row):
        return lax.dynamic_slice_in_dim(row, side * half_heads, half_heads, 0)

    fade_own = jnp.exp(cum[-1])
    lanes = jnp.pad(cum[-1:], ((0, 0), (0, -heads % 128)))
    fade_other = jnp.exp(send(lanes, pair(count))[0, :heads])
    ones = jnp.ones_like(fade_own)
    chip_weights = jnp.stack(
        [
            side_half(jnp.where(side == 0, fade_other, ones)),
            side_half(jnp.where(side == 0, ones, fade_own)),
        ]
    )
    enter_weights = jnp.stack(
        [jnp.where(side == 0, ones, fade_other), jnp.where(side == 0, 0.0, ones)]
    )

    cum_mine = lax.dynamic_slice_in_dim(cum, side * half_heads, half_heads, 1)
    cum_theirs = lax.dynamic_slice_in_dim(cum, (1 - side) * half_heads, half_heads, 1)
    state_theirs = local_states(keys, values, cum_theirs, 1 - side)
    state_mine = local_states(keys, values, cum_mine, side)
    other_mine = send(state_theirs, pair(count))
    other_theirs = send(state_mine, pair(count))
    chip = combine([state_mine, other_mine], chip_weights)
    within, act = within_block(queries, keys, values, out_gate, after(cum, chip), head_gain)
    held, names = [chip], [me]
    for step in range(steps - 1):
        got = send(jnp.stack(held) if step else held[0][None], hop(count, step))
        mask = hop_mask(count, step, side)
        held = held + [got[i] for i in range(len(held))]
        names = names + [name ^ mask for name in names]
    there = me ^ hop_mask(count, steps - 1, side)
    towards = [jnp.stack([side_half(faded(name, t)) for name in names]) for t in (there, me)]
    got = send(combine(held, after(towards[0], within)), hop(count, steps - 1))
    alone = jnp.concatenate([towards[1], jnp.ones((1, half_heads), F32)])
    entering = combine(held + [got], alone)
    states = [entering, send(entering, pair(count)), other_mine, other_theirs]
    halves = 2
    each = seqs // halves
    mixed = [
        mixed_rows(
            queries, states, enter_weights, side, within, act, cum, sub, h * each, each
        ).reshape(parts * each * sub, width)
        for h in range(halves)
    ]

    summed = []
    gates = [(), tuple(mixed[1:])]
    for h in range(halves):
        pieces = spread(mixed[h], count, gates)
        partial = project(pieces, out_weight, order_array, parts)
        gates = [(pieces[1],)] + [()] * (steps - 1) + [(partial,)]
        summed.append(lax.psum_scatter(partial, "exp", scatter_dimension=0))

    stream_rows = after(stream, partial).reshape(tokens, model)
    stream_got = swap_blocks(cut_columns(stream_rows, mates), count)
    residual, square = residual_sums(mates, stream_got, summed)
    residual = residual.reshape(count * tokens, cols)

    square = sum_over(square.reshape(count * tokens), count)
    scale = lax.rsqrt(square / model + 1e-06)
    gain = lax.dynamic_slice_in_dim(norm_gain, me * cols, cols, 0)
    rows_in = (residual * scale[:, None] * gain).astype(BF)

    expert_local = w_gate.shape[0]
    experts = expert_local * parts
    capacity = max(2, (2 * tokens + experts - 1) // experts + 1)
    one_hot = ids[:, :, None] == jnp.arange(experts, dtype=jnp.int32)
    earlier = jnp.arange(2 * tokens)[:, None] > jnp.arange(2 * tokens)[None, :]
    ahead = jnp.einsum(
        "tu,gue->gte", earlier.astype(BF), one_hot.astype(BF), preferred_element_type=F32
    )
    ranking = jnp.sum(jnp.where(one_hot, ahead, 0.0), axis=2).astype(jnp.int32)
    slots = capacity * count
    turned = (ids - mine + experts) % experts
    slot_of = (turned * count + jnp.arange(count, dtype=jnp.int32)[:, None]) * capacity + ranking
    slot_of = slot_of.reshape(count * tokens, 2)
    share_of = shares.reshape(count * tokens, 2)
    sent = []
    for turn in range(parts):
        numbers = turn * slots + jnp.arange(slots, dtype=jnp.int32)
        hit = [slot_of[:, k][None, :] == numbers[:, None] for k in range(2)]
        placing = hit[0] | hit[1]
        dispatch = jnp.dot(placing.astype(BF), rows_in, preferred_element_type=F32).astype(BF)
        if turn:
            dispatch = lax.ppermute(dispatch, "exp", [(i, (i + turn) % parts) for i in range(parts)])
        sent.append(dispatch)

    arrived = []
    for turn in range(parts):
        gates = [()] * steps
        if turn == 0:
            gates[-1] = (sent[1],)
        elif turn == 1:
            gates[-1] = (arrived[0][steps], sent[2 % parts])
            gates.append((sent[3 % parts],))
        else:
            gates[0] = (arrived[0 if turn < 4 else turn - 2][steps],)
        arrived.append(spread(sent[turn], count, gates))
    near_order, far_order = order_array[: count // 2], order_array[count // 2 :]
    returned = []
    waits, moved = [], [[]] * steps
    for first in range(0, parts, 2):
        turns = range(first, min(first + 2, parts))
        later = range(first + 2, min(first + 4, parts))
        ready = [arrived[t][1] for t in later]
        groups = [arrived[t] for t in turns]
        groups[0] = list(after(tuple(groups[0]), *waits, *ready))
        hidden = hidden_units(groups, w_gate[0], w_up[0], order_array)
        ready = [arrived[t][steps] for t in later]
        far = down_blocks(after(tuple(hidden), *ready, *moved[0]), w_down[0], far_order)
        ready = [arrived[t][-1] for t in later]
        near = down_blocks(after(tuple(hidden), *far, *ready, *moved[-1]), w_down[0], near_order)
        waits = totals = [pair_sum(n, f, count) for n, f in zip(near, far)]
        moved = [[] for _ in range(steps)]
        before = ()
        for turn, total in zip(turns, totals):
            done, got = gathered_sum(total, count, (before,))
            for step in range(steps):
                moved[step].append(got[step])
            if first + 2 >= parts:
                before = (got[0],)
            if turn:
                back = [((i + turn) % parts, i) for i in range(parts)]
                done = lax.ppermute(done, "exp", back)
            returned.append(done)
    result = residual
    for turn in range(parts):
        numbers = turn * slots + jnp.arange(slots, dtype=jnp.int32)
        weighting = sum(
            jnp.where(slot_of[:, k][:, None] == numbers[None, :], share_of[:, k][:, None], 0.0)
            for k in range(2)
        )
        high = weighting.astype(BF)
        low = (weighting - high.astype(F32)).astype(BF)
        result = result + jnp.dot(high, returned[turn], preferred_element_type=F32)
        result = result + jnp.dot(low, returned[turn], preferred_element_type=F32)
    result = result.astype(BF).reshape(count, tokens, cols)
    blocks = [lax.dynamic_index_in_dim(result, me ^ j, 0, False) for j in range(count)]
    return lay_columns(swap_blocks(blocks, count), mates).reshape(seqs, sub, model)


def solution(mesh):
    return jax.shard_map(
        body,
        mesh=mesh,
        in_specs=(
            P(None, "ctx", "exp"),
            P(None, "ctx", "exp"),
            P(None, "ctx", "exp"),
            P("ctx", "exp"),
            P(None, "ctx", "exp"),
            P("exp"),
            P("exp", "ctx"),
            P(None, ("ctx", "exp"), None),
            P(),
            P(("ctx", "exp"), None, None),
            P(("ctx", "exp"), None, None),
            P("exp", None, "ctx"),
            P("exp", None, "ctx"),
            P("exp", "ctx", None),
        ),
        out_specs=P(None, ("ctx", "exp"), None),
        check_vma=False,
    )
```

```python
import functools

import jax
import jax.numpy as jnp
from jax import lax
from jax.experimental import pallas as pl
from jax.experimental.pallas import tpu as pltpu
from jax.sharding import PartitionSpec as P

MIB = 1 << 20
BF = jnp.bfloat16
F32 = jnp.float32


def routes(count):
    bits = [1 << b for b in range(1, count.bit_length() - 1)]
    turn = len(bits) // 2
    return bits, bits[turn:] + bits[:turn]


def hop(count, step):
    both = routes(count)
    return [(i, i ^ both[i & 1][step]) for i in range(count)]


def hop_mask(count, step, side):
    both = routes(count)
    return jnp.where(side == 0, both[0][step], both[1][step])


def pair(count):
    return [(i, i ^ 1) for i in range(count)]


def held_by(count, who):
    held = [who]
    for step in range(len(routes(count)[0])):
        mask = hop_mask(count, step, who & 1)
        held = held + [h ^ mask for h in held]
    return held


def block_order(count, me):
    return held_by(count, me) + held_by(count, me ^ 1)


def send(x, perm):
    return lax.ppermute(x, "ctx", perm)


def after(x, *others):
    return lax.optimization_barrier((x, *others))[0]


def joined(parts):
    return parts[0] if len(parts) == 1 else jnp.concatenate(parts, axis=0)


def spread(x, count, gates=()):
    pieces = [x[None]]
    for step in range(len(routes(count)[0])):
        block = joined(pieces)
        if step < len(gates):
            block = after(block, *gates[step])
        pieces.append(send(block, hop(count, step)))
    block = tuple(pieces)
    if len(gates) > len(routes(count)[0]):
        block = after(block, *gates[-1])
    return pieces + [send(x, pair(count)) for x in block]


def halved_sum(x, other):
    half = max(1, x.shape[0] // 2)

    def added(at):
        return (x[at].astype(F32) + other[at].astype(F32)).astype(BF)

    if x.shape[0] == 1:
        return added(slice(0, 1)), None
    return added(slice(0, half)), added(slice(half, None))


def pair_sum(near, far, count):
    return halved_sum(near, send(far, pair(count)))


def gathered_sum(total, count, gates=()):
    got = []
    stays, leaves = total
    for at, step in enumerate(reversed(range(len(routes(count)[0])))):
        if at < len(gates):
            leaves = after(leaves, *gates[at])
        got.append(send(leaves, hop(count, step)))
        stays, leaves = halved_sum(stays, got[-1])
    return stays[0], got


def sum_over(x, count):
    for bit in range(count.bit_length() - 1):
        x = x + send(x, [(i, i ^ (1 << bit)) for i in range(count)])
    return x


def swap_blocks(blocks, count):
    got = [blocks[0]]
    for j in range(1, count):
        got.append(send(blocks[j], [(i, i ^ j) for i in range(count)]))
    return got


def cut_kernel(mates_ref, x_ref, *outs):
    cols = outs[0].shape[1]
    for j, out in enumerate(outs):
        out[...] = x_ref[:, pl.ds(pl.multiple_of(mates_ref[j] * cols, cols), cols)]


def cut_columns(x, mates):
    rows, width = x.shape
    count = mates.shape[0]
    whole = pl.BlockSpec(memory_space=pltpu.VMEM)
    shape = jax.ShapeDtypeStruct((rows, width // count), x.dtype)
    return pl.pallas_call(
        cut_kernel,
        in_specs=[pl.BlockSpec(memory_space=pltpu.SMEM), whole],
        out_specs=[whole] * count,
        out_shape=[shape] * count,
    )(mates, x)


def lay_kernel(mates_ref, *refs):
    *blocks, out_ref = refs
    cols = blocks[0].shape[1]
    for j, ref in enumerate(blocks):
        out_ref[:, pl.ds(pl.multiple_of(mates_ref[j] * cols, cols), cols)] = ref[...]


def lay_columns(blocks, mates):
    rows, cols = blocks[0].shape
    whole = pl.BlockSpec(memory_space=pltpu.VMEM)
    return pl.pallas_call(
        lay_kernel,
        in_specs=[pl.BlockSpec(memory_space=pltpu.SMEM)] + [whole] * len(blocks),
        out_specs=whole,
        out_shape=jax.ShapeDtypeStruct((rows, cols * len(blocks)), blocks[0].dtype),
    )(mates, *blocks)


def state_kernel(dim, place_ref, k_ref, v_ref, cum_ref, out_ref):
    cum = cum_ref[...]
    fade = jnp.exp(cum[-1:, :] - cum)
    for h in range(cum.shape[1]):
        lanes = slice(h * dim, (h + 1) * dim)
        faded = (k_ref[0, :, lanes].astype(F32) * fade[:, h : h + 1]).astype(BF)
        out_ref[0, h] = lax.dot_general(
            faded, v_ref[0, :, lanes], (((0,), (0,)), ((), ())), preferred_element_type=F32
        ).astype(BF)


def local_states(keys, values, cum, place, first, seqs):
    _, block, width = keys.shape
    heads = cum.shape[1]
    dim = width // 2 // heads
    rows = pl.BlockSpec((1, block, width // 2), lambda s, place: (s + first, 0, place[0]))
    return pl.pallas_call(
        functools.partial(state_kernel, dim),
        grid_spec=pltpu.PrefetchScalarGridSpec(
            num_scalar_prefetch=1,
            grid=(seqs,),
            in_specs=[rows, rows, pl.BlockSpec((block, heads), lambda s, place: (0, 0))],
            out_specs=pl.BlockSpec((1, heads, dim, dim), lambda s, place: (s, 0, 0, 0)),
        ),
        out_shape=jax.ShapeDtypeStruct((seqs, heads, dim, dim), BF),
        compiler_params=pltpu.CompilerParams(vmem_limit_bytes=60 * MIB),
        cost_estimate=pl.CostEstimate(
            flops=2000000000, bytes_accessed=2 * seqs * width * (block + dim), transcendentals=0
        ),
    )(place.reshape(1).astype(jnp.int32), keys, values, cum)


def within_kernel(dim, q_ref, k_ref, v_ref, g_ref, cum_ref, cumt_ref, gain_ref, out_ref, act_ref):
    cum = cum_ref[...]
    block = cum.shape[0]
    causal = lax.broadcasted_iota(jnp.int32, (block, block), 0) >= lax.broadcasted_iota(
        jnp.int32, (block, block), 1
    )
    for h in range(cum.shape[1]):
        lanes = slice(h * dim, (h + 1) * dim)
        scores = lax.dot_general(
            q_ref[0, :, lanes],
            k_ref[0, :, lanes],
            (((1,), (1,)), ((), ())),
            preferred_element_type=F32,
        )
        gap = jnp.where(causal, cum[:, h : h + 1] - cumt_ref[h : h + 1, :], -1e30)
        weights = (scores * jnp.exp(gap)).astype(BF)
        out_ref[0, :, lanes] = jnp.dot(weights, v_ref[0, :, lanes], preferred_element_type=F32)
    act_ref[0] = gain_ref[...] * jax.nn.sigmoid(g_ref[0].astype(F32))


def within_block(queries, keys, values, gate, cum, head_gain, first, seqs):
    _, block, width = keys.shape
    heads = cum.shape[1]
    dim = width // heads
    rows = pl.BlockSpec((1, block, width), lambda s: (s + first, 0, 0))
    out = pl.BlockSpec((1, block, width), lambda s: (s, 0, 0))
    shape = jax.ShapeDtypeStruct((seqs, block, width), F32)
    return pl.pallas_call(
        functools.partial(within_kernel, dim),
        grid=(seqs,),
        in_specs=[
            rows,
            rows,
            rows,
            rows,
            pl.BlockSpec((block, heads), lambda s: (0, 0)),
            pl.BlockSpec((heads, block), lambda s: (0, 0)),
            pl.BlockSpec((1, width), lambda s: (0, 0)),
        ],
        out_specs=[out, out],
        out_shape=[shape, shape],
        compiler_params=pltpu.CompilerParams(vmem_limit_bytes=60 * MIB),
        cost_estimate=pl.CostEstimate(
            flops=60 * seqs * block * block * width,
            bytes_accessed=16 * seqs * block * width,
            transcendentals=seqs * block * width,
        ),
    )(queries, keys, values, gate, cum, cum.T, head_gain[None])


def combine_kernel(weight_ref, *refs):
    *states, out_ref = refs
    for h in range(out_ref.shape[1]):
        out_ref[0, h] = sum(
            weight_ref[i, h] * ref[0, h].astype(F32) for i, ref in enumerate(states)
        ).astype(BF)


def combine(states, weights):
    seqs, heads, dim, _ = states[0].shape
    block = pl.BlockSpec((1, heads, dim, dim), lambda s: (s, 0, 0, 0))
    return pl.pallas_call(
        combine_kernel,
        grid=(seqs,),
        in_specs=[pl.BlockSpec(memory_space=pltpu.SMEM)] + [block] * len(states),
        out_specs=block,
        out_shape=jax.ShapeDtypeStruct(states[0].shape, BF),
        compiler_params=pltpu.CompilerParams(vmem_limit_bytes=16 * MIB),
    )(weights, *states)


def mixed_kernel(
    dim, sub, side_ref, weight_ref, q_ref, own_ref, got_ref, pair_own_ref, pair_got_ref,
    within_ref, act_ref, cum_ref, out_ref,
):
    scale = jnp.exp(cum_ref[...])
    heads = scale.shape[1]
    half = heads // 2
    for h in range(heads):
        lanes = slice(h * dim, (h + 1) * dim)
        here = side_ref[0] == h // half
        entering = jnp.where(here, own_ref[0, h % half], got_ref[0, h % half]).astype(F32)
        paired = jnp.where(here, pair_own_ref[0, h % half], pair_got_ref[0, h % half]).astype(F32)
        state = (weight_ref[0, h] * entering + weight_ref[1, h] * paired).astype(BF)
        carried = jnp.dot(q_ref[0, :, lanes], state, preferred_element_type=F32)
        attended = within_ref[0, :, lanes] + carried * scale[:, h : h + 1]
        square = jnp.mean(attended * attended, axis=1, keepdims=True)
        mixed = (attended * lax.rsqrt(square + 1e-06) * act_ref[0, :, lanes]).astype(BF)
        for d in range(out_ref.shape[0]):
            out_ref[d, 0, :, lanes] = mixed[d * sub : (d + 1) * sub]


def mixed_rows(queries, states, weights, side, within, act, cum, sub, first, seqs):
    _, block, width = queries.shape
    heads = cum.shape[1]
    dim = width // heads
    parts = block // sub
    rows = pl.BlockSpec((1, block, width), lambda s, side: (s + first, 0, 0))
    here = pl.BlockSpec((1, block, width), lambda s, side: (s, 0, 0))
    halved = pl.BlockSpec((1, heads // 2, dim, dim), lambda s, side: (s, 0, 0, 0))
    return pl.pallas_call(
        functools.partial(mixed_kernel, dim, sub),
        grid_spec=pltpu.PrefetchScalarGridSpec(
            num_scalar_prefetch=1,
            grid=(seqs,),
            in_specs=[pl.BlockSpec(memory_space=pltpu.SMEM), rows]
            + [halved] * 4
            + [here, here, pl.BlockSpec((block, heads), lambda s, side: (0, 0))],
            out_specs=pl.BlockSpec((parts, 1, sub, width), lambda s, side: (0, s, 0, 0)),
        ),
        out_shape=jax.ShapeDtypeStruct((parts, seqs, sub, width), BF),
        compiler_params=pltpu.CompilerParams(vmem_limit_bytes=60 * MIB),
        cost_estimate=pl.CostEstimate(
            flops=6000000000, bytes_accessed=14 * seqs * block * width, transcendentals=0
        ),
    )(side.reshape(1).astype(jnp.int32), weights, queries, *states, within, act, cum)


def project_kernel(sizes, order_ref, *refs):
    *pieces, w_ref, out_ref = refs
    parts, _, rows, _ = out_ref.shape
    at = 0
    for ref, size in zip(pieces, sizes):
        for i in range(size):
            product = jnp.dot(ref[i], w_ref[...], preferred_element_type=F32).astype(BF)
            for d in range(parts):
                out_ref[d, order_ref[at]] = product[d * rows : (d + 1) * rows]
            at += 1


def project(pieces, weight, order, parts):
    count = sum(p.shape[0] for p in pieces)
    rows, depth = pieces[0].shape[1:]
    cols = weight.shape[1]
    whole = pl.BlockSpec(memory_space=pltpu.VMEM)
    return pl.pallas_call(
        functools.partial(project_kernel, [p.shape[0] for p in pieces]),
        in_specs=[pl.BlockSpec(memory_space=pltpu.SMEM)] + [whole] * (len(pieces) + 1),
        out_specs=whole,
        out_shape=jax.ShapeDtypeStruct((parts, count, rows // parts, cols), BF),
        compiler_params=pltpu.CompilerParams(vmem_limit_bytes=20 * MIB),
        cost_estimate=pl.CostEstimate(
            flops=4 * count * rows * depth * cols,
            bytes_accessed=2 * (count * rows * (depth + cols) + depth * cols),
            transcendentals=0,
        ),
    )(order, *pieces, weight)


def residual_kernel(count, mates_ref, *refs):
    stream, sums = refs[:count], refs[count:-2]
    out_ref, square_ref = refs[-2:]
    rows = out_ref.shape[1] // len(sums)
    for j in range(count):
        out_ref[mates_ref[j]] = stream[j][...].astype(F32)
    for b in range(count):
        for h, ref in enumerate(sums):
            at = slice(h * rows, (h + 1) * rows)
            total = out_ref[b, at] + ref[b].astype(F32)
            out_ref[b, at] = total
            square_ref[b, at] = jnp.sum(total * total, axis=1, keepdims=True)


def residual_sums(mates, stream, sums):
    count = len(stream)
    rows, cols = stream[0].shape
    whole = pl.BlockSpec(memory_space=pltpu.VMEM)
    return pl.pallas_call(
        functools.partial(residual_kernel, count),
        in_specs=[pl.BlockSpec(memory_space=pltpu.SMEM)] + [whole] * (count + len(sums)),
        out_specs=[whole] * 2,
        out_shape=[
            jax.ShapeDtypeStruct((count, rows, cols), F32),
            jax.ShapeDtypeStruct((count, rows, 1), F32),
        ],
        compiler_params=pltpu.CompilerParams(vmem_limit_bytes=32 * MIB),
    )(mates, *stream, *sums)


def hidden_kernel(sizes, groups, order_ref, *refs):
    steps = sum(sizes)
    each = len(sizes)
    pieces = [refs[g * each : (g + 1) * each] for g in range(groups)]
    refs = refs[groups * each :]
    (gate_ref, up_ref), outs = refs[:2], refs[2:]
    outs, g_acc, u_acc = outs[:groups], outs[-2], outs[-1]
    i = pl.program_id(0)
    hid = gate_ref.shape[1]
    main = hid - 128 if hid % 256 == 128 else hid

    def products(rows):
        for acc, ref in ((g_acc, gate_ref), (u_acc, up_ref)):
            yield acc, slice(0, main), jnp.dot(rows, ref[:, :main], preferred_element_type=F32)
        if main < hid:
            rest = jnp.concatenate([gate_ref[:, main:], up_ref[:, main:]], axis=1)
            both = jnp.dot(rows, rest, preferred_element_type=F32)
            yield g_acc, slice(main, hid), both[:, : hid - main]
            yield u_acc, slice(main, hid), both[:, hid - main :]

    start = 0
    for p, size in enumerate(sizes):

        @pl.when((i >= start) & (i < start + size))
        def _(p=p, start=start):
            for g in range(groups):
                rows = pieces[g][p][0]
                for acc, at, product in products(rows):
                    if start == 0:
                        acc[g, :, at] = product
                    else:
                        acc[g, :, at] += product

        start += size

    @pl.when(i == steps - 1)
    def _():
        for g in range(groups):
            v = g_acc[g]
            outs[g][...] = (v / (1.0 + jnp.exp(-v)) * u_acc[g]).astype(BF)


def hidden_units(groups, w_gate, w_up, order):
    sizes = [p.shape[0] for p in groups[0]]
    rows, cols = groups[0][0].shape[1:]
    depth, hid = w_gate.shape
    many = len(groups)
    specs = []
    start = 0
    for size in sizes:
        specs.append(
            pl.BlockSpec(
                (1, rows, cols),
                lambda i, order, start=start, size=size: (jnp.clip(i - start, 0, size - 1), 0, 0),
            )
        )
        start += size
    up_spec = pl.BlockSpec((cols, hid), lambda i, order: (order[i], 0))
    return pl.pallas_call(
        functools.partial(hidden_kernel, sizes, many),
        grid_spec=pltpu.PrefetchScalarGridSpec(
            num_scalar_prefetch=1,
            grid=(sum(sizes),),
            in_specs=specs * many
            + [up_spec, up_spec],
            out_specs=[pl.BlockSpec((rows, hid), lambda i, order: (0, 0))] * many,
            scratch_shapes=[pltpu.VMEM((many, rows, hid), F32)] * 2,
        ),
        out_shape=[jax.ShapeDtypeStruct((rows, hid), BF)] * many,
        compiler_params=pltpu.CompilerParams(vmem_limit_bytes=60 * MIB),
        cost_estimate=pl.CostEstimate(
            flops=8 * many * rows * depth * hid,
            bytes_accessed=4 * depth * hid + 2 * many * rows * depth,
            transcendentals=many * rows * hid,
        ),
    )(order, *[p for pieces in groups for p in pieces], w_gate, w_up)


def down_kernel(groups, order_ref, *refs):
    hidden, weight, outs = refs[:groups], refs[groups], refs[groups + 1 :]
    for g in range(groups):
        outs[g][0] = jnp.dot(hidden[g][...], weight[...], preferred_element_type=F32).astype(BF)


def down_blocks(hidden, w_down, order):
    many = len(hidden)
    rows, hid = hidden[0].shape
    blocks, model = order.shape[0], w_down.shape[1]
    cols = model // lax.axis_size("ctx")

    return pl.pallas_call(
        functools.partial(down_kernel, many),
        grid_spec=pltpu.PrefetchScalarGridSpec(
            num_scalar_prefetch=1,
            grid=(blocks,),
            in_specs=[pl.BlockSpec((rows, hid), lambda i, order: (0, 0))] * many
            + [pl.BlockSpec((hid, cols), lambda i, order: (0, order[i]))],
            out_specs=[pl.BlockSpec((1, rows, cols), lambda i, order: (i, 0, 0))] * many,
        ),
        out_shape=[jax.ShapeDtypeStruct((blocks, rows, cols), BF)] * many,
        compiler_params=pltpu.CompilerParams(vmem_limit_bytes=60 * MIB),
        cost_estimate=pl.CostEstimate(
            flops=4 * many * rows * cols * blocks * hid,
            bytes_accessed=2 * cols * blocks * hid + 2 * many * rows * cols * blocks,
            transcendentals=0,
        ),
    )(order, *hidden, w_down)


def body(
    queries,
    keys,
    values,
    decay_log,
    out_gate,
    head_gain,
    out_weight,
    stream,
    norm_gain,
    expert_ids,
    expert_share,
    w_gate,
    w_up,
    w_down,
):
    count = lax.axis_size("ctx")
    parts = lax.axis_size("exp")
    me = lax.axis_index("ctx")
    mine = lax.axis_index("exp")
    side = me & 1
    seqs, block, width = queries.shape
    heads = decay_log.shape[1]
    sub, model = stream.shape[1:]
    tokens = seqs * sub
    cols = model // count
    order = block_order(count, me)
    order_array = jnp.stack(order).astype(jnp.int32)

    cum = jnp.cumsum(decay_log, axis=0)
    small = jnp.concatenate(
        [
            expert_ids.reshape(2 * tokens).astype(F32),
            expert_share.reshape(2 * tokens),
            cum[-1],
        ]
    )
    cum_mine = lax.dynamic_slice_in_dim(cum, side * (heads // 2), heads // 2, 1)
    cum_theirs = lax.dynamic_slice_in_dim(cum, (1 - side) * (heads // 2), heads // 2, 1)
    halves = 2
    each = seqs // halves
    state_theirs = local_states(keys, values, cum_theirs, 1 - side, 0, each)
    small = jnp.pad(small, (0, -small.shape[0] % 128)).reshape(-1, 128)
    facts = joined(spread(after(small, state_theirs), count)).reshape(count, -1)
    steps = len(routes(count)[0])
    place = order_array[None, :] == jnp.arange(count, dtype=jnp.int32)[:, None]
    facts = jnp.sum(jnp.where(place[:, :, None], facts[None], 0.0), axis=1)
    ids = facts[:, : 2 * tokens].astype(jnp.int32)
    shares = facts[:, 2 * tokens : 4 * tokens]
    ends = facts[:, 4 * tokens : 4 * tokens + heads]

    mates = (me ^ jnp.arange(count, dtype=jnp.int32)).astype(jnp.int32)

    block_no = jnp.arange(count)

    def faded(source, target):
        between = (block_no >= 2 * (source // 2 + 1)) & (block_no < 2 * (target // 2))
        power = jnp.sum(jnp.where(between[:, None], ends, 0.0), axis=0)
        return jnp.where(source // 2 < target // 2, jnp.exp(power), 0.0)

    half_heads = heads // 2

    def side_half(row):
        return lax.dynamic_slice_in_dim(row, side * half_heads, half_heads, 0)

    fade_own = jnp.exp(cum[-1])
    lanes = jnp.pad(cum[-1:], ((0, 0), (0, -heads % 128)))
    fade_other = jnp.exp(send(lanes, pair(count))[0, :heads])
    ones = jnp.ones_like(fade_own)
    chip_weights = jnp.stack(
        [
            side_half(jnp.where(side == 0, fade_other, ones)),
            side_half(jnp.where(side == 0, ones, fade_own)),
        ]
    )
    enter_weights = jnp.stack(
        [jnp.where(side == 0, ones, fade_other), jnp.where(side == 0, 0.0, ones)]
    )

    there = me ^ hop_mask(count, steps - 1, side)
    summed = []
    arrivals, mixed, spreads = (), None, ()
    for h in range(halves):
        first = h * each
        if h:
            state_theirs = local_states(
                keys, values, after(cum_theirs, *arrivals[:1]), 1 - side, first, each
            )
        state_mine = local_states(
            keys, values, after(cum_mine, *arrivals[:1]), side, first, each
        )
        other_mine = send(state_theirs, pair(count))
        other_theirs = send(state_mine, pair(count))
        chip = combine([state_mine, other_mine], chip_weights)
        within, act = within_block(
            queries,
            keys,
            values,
            out_gate,
            after(cum, chip if mixed is None else mixed),
            head_gain,
            first,
            each,
        )
        held, names = [after(chip, *arrivals[1:])], [me]
        for step in range(steps - 1):
            got = send(jnp.stack(held) if step else held[0][None], hop(count, step))
            mask = hop_mask(count, step, side)
            held = held + [got[i] for i in range(len(held))]
            names = names + [name ^ mask for name in names]
        towards = [jnp.stack([side_half(faded(name, t)) for name in names]) for t in (there, me)]
        leaving = combine(held, after(towards[0], within, *spreads[1:2]))
        got = send(leaving, hop(count, steps - 1))
        arrivals = (held[-1], got)
        alone = jnp.concatenate([towards[1], jnp.ones((1, half_heads), F32)])
        entering = combine(held + [got], alone)
        states = [entering, send(entering, pair(count)), other_mine, other_theirs]
        mixed = mixed_rows(
            queries, states, enter_weights, side, within, act, cum, sub, first, each
        )
        gates = [spreads[2:3]] + [()] * (steps - 1) + [(partial,)] if h else ()
        pieces = spread(mixed.reshape(parts * each * sub, width), count, gates)
        partial = project(pieces, out_weight, order_array, parts)
        spreads = tuple(pieces)
        summed.append(lax.psum_scatter(partial, "exp", scatter_dimension=0))

    stream_rows = after(stream, partial).reshape(tokens, model)
    stream_got = swap_blocks(cut_columns(stream_rows, mates), count)
    residual, square = residual_sums(mates, stream_got, summed)
    residual = residual.reshape(count * tokens, cols)

    square = sum_over(square.reshape(count * tokens), count)
    scale = lax.rsqrt(square / model + 1e-06)
    gain = lax.dynamic_slice_in_dim(norm_gain, me * cols, cols, 0)
    rows_in = (residual * scale[:, None] * gain).astype(BF)

    expert_local = w_gate.shape[0]
    experts = expert_local * parts
    capacity = max(2, (2 * tokens + experts - 1) // experts + 1)
    one_hot = ids[:, :, None] == jnp.arange(experts, dtype=jnp.int32)
    earlier = jnp.arange(2 * tokens)[:, None] > jnp.arange(2 * tokens)[None, :]
    ahead = jnp.einsum(
        "tu,gue->gte", earlier.astype(BF), one_hot.astype(BF), preferred_element_type=F32
    )
    ranking = jnp.sum(jnp.where(one_hot, ahead, 0.0), axis=2).astype(jnp.int32)
    slots = capacity * count
    turned = (ids - mine + experts) % experts
    slot_of = (turned * count + jnp.arange(count, dtype=jnp.int32)[:, None]) * capacity + ranking
    slot_of = slot_of.reshape(count * tokens, 2)
    share_of = shares.reshape(count * tokens, 2)
    sent = []
    for turn in range(parts):
        numbers = turn * slots + jnp.arange(slots, dtype=jnp.int32)
        hit = [slot_of[:, k][None, :] == numbers[:, None] for k in range(2)]
        placing = hit[0] | hit[1]
        dispatch = jnp.dot(placing.astype(BF), rows_in, preferred_element_type=F32).astype(BF)
        if turn:
            dispatch = lax.ppermute(dispatch, "exp", [(i, (i + turn) % parts) for i in range(parts)])
        sent.append(dispatch)

    arrived = []
    for turn in range(parts):
        gates = [()] * steps
        if turn == 0:
            gates[-1] = (sent[1],)
        elif turn == 1:
            gates[-1] = (arrived[0][steps], sent[2 % parts])
            gates.append((sent[3 % parts],))
        else:
            gates[0] = (arrived[0 if turn < 4 else turn - 2][steps],)
        arrived.append(spread(sent[turn], count, gates))
    near_order, far_order = order_array[: count // 2], order_array[count // 2 :]
    returned = []
    waits, moved = [], [[]] * steps
    for first in range(0, parts, 2):
        turns = range(first, min(first + 2, parts))
        later = range(first + 2, min(first + 4, parts))
        ready = [arrived[t][1] for t in later]
        groups = [arrived[t] for t in turns]
        groups[0] = list(after(tuple(groups[0]), *waits, *ready))
        hidden = hidden_units(groups, w_gate[0], w_up[0], order_array)
        ready = [arrived[t][steps] for t in later]
        far = down_blocks(after(tuple(hidden), *ready, *moved[0]), w_down[0], far_order)
        ready = [arrived[t][-1] for t in later]
        near = down_blocks(after(tuple(hidden), *far, *ready), w_down[0], near_order)
        totals = [pair_sum(n, f, count) for n, f in zip(near, far)]
        waits = [leaves for _, leaves in totals]
        before = tuple(moved[-1])
        moved = [[] for _ in range(steps)]
        for turn, total in zip(turns, totals):
            done, got = gathered_sum(total, count, (before,))
            for step in range(steps):
                moved[step].append(got[step])
            if first + 2 >= parts:
                before = (got[0],)
            if turn:
                back = [((i + turn) % parts, i) for i in range(parts)]
                done = lax.ppermute(done, "exp", back)
            returned.append(done)
    result = residual
    for turn in range(parts):
        numbers = turn * slots + jnp.arange(slots, dtype=jnp.int32)
        weighting = sum(
            jnp.where(slot_of[:, k][:, None] == numbers[None, :], share_of[:, k][:, None], 0.0)
            for k in range(2)
        )
        high = weighting.astype(BF)
        low = (weighting - high.astype(F32)).astype(BF)
        result = result + jnp.dot(high, returned[turn], preferred_element_type=F32)
        result = result + jnp.dot(low, returned[turn], preferred_element_type=F32)
    result = result.astype(BF).reshape(count, tokens, cols)
    blocks = [lax.dynamic_index_in_dim(result, me ^ j, 0, False) for j in range(count)]
    return lay_columns(swap_blocks(blocks, count), mates).reshape(seqs, sub, model)


def solution(mesh):
    return jax.shard_map(
        body,
        mesh=mesh,
        in_specs=(
            P(None, "ctx", "exp"),
            P(None, "ctx", "exp"),
            P(None, "ctx", "exp"),
            P("ctx", "exp"),
            P(None, "ctx", "exp"),
            P("exp"),
            P("exp", "ctx"),
            P(None, ("ctx", "exp"), None),
            P(),
            P(("ctx", "exp"), None, None),
            P(("ctx", "exp"), None, None),
            P("exp", None, "ctx"),
            P("exp", None, "ctx"),
            P("exp", "ctx", None),
        ),
        out_specs=P(None, ("ctx", "exp"), None),
        check_vma=False,
    )
```

```python
import functools

import jax
import jax.numpy as jnp
from jax import lax
from jax.experimental import pallas as pl
from jax.experimental.pallas import tpu as pltpu
from jax.sharding import PartitionSpec as P

MIB = 1 << 20
BF = jnp.bfloat16
F32 = jnp.float32


def routes(count):
    bits = [1 << b for b in range(1, count.bit_length() - 1)]
    turn = len(bits) // 2
    return bits, bits[turn:] + bits[:turn]


def hop(count, step):
    both = routes(count)
    return [(i, i ^ both[i & 1][step]) for i in range(count)]


def hop_mask(count, step, side):
    both = routes(count)
    return jnp.where(side == 0, both[0][step], both[1][step])


def pair(count):
    return [(i, i ^ 1) for i in range(count)]


def held_by(count, who):
    held = [who]
    for step in range(len(routes(count)[0])):
        mask = hop_mask(count, step, who & 1)
        held = held + [h ^ mask for h in held]
    return held


def block_order(count, me):
    return held_by(count, me) + held_by(count, me ^ 1)


def send(x, perm):
    return lax.ppermute(x, "ctx", perm)


def after(x, *others):
    return lax.optimization_barrier((x, *others))[0]


def joined(parts):
    return parts[0] if len(parts) == 1 else jnp.concatenate(parts, axis=0)


def spread(x, count, gates=()):
    pieces = [x[None]]
    for step in range(len(routes(count)[0])):
        block = joined(pieces)
        if step < len(gates):
            block = after(block, *gates[step])
        pieces.append(send(block, hop(count, step)))
    block = tuple(pieces)
    if len(gates) > len(routes(count)[0]):
        block = after(block, *gates[-1])
    return pieces + [send(x, pair(count)) for x in block]


def halved_sum(x, other):
    half = max(1, x.shape[0] // 2)

    def added(at):
        return (x[at].astype(F32) + other[at].astype(F32)).astype(BF)

    if x.shape[0] == 1:
        return added(slice(0, 1)), None
    return added(slice(0, half)), added(slice(half, None))


def pair_sum(near, far, count):
    return halved_sum(near, send(far, pair(count)))


def gathered_sum(total, count, gates=()):
    got = []
    stays, leaves = total
    for at, step in enumerate(reversed(range(len(routes(count)[0])))):
        if at < len(gates):
            leaves = after(leaves, *gates[at])
        got.append(send(leaves, hop(count, step)))
        stays, leaves = halved_sum(stays, got[-1])
    return stays[0], got


def sum_over(x, count):
    for bit in range(count.bit_length() - 1):
        x = x + send(x, [(i, i ^ (1 << bit)) for i in range(count)])
    return x


def swap_blocks(blocks, count):
    got = [blocks[0]]
    for j in range(1, count):
        got.append(send(blocks[j], [(i, i ^ j) for i in range(count)]))
    return got


def cut_kernel(mates_ref, x_ref, *outs):
    cols = outs[0].shape[1]
    for j, out in enumerate(outs):
        out[...] = x_ref[:, pl.ds(pl.multiple_of(mates_ref[j] * cols, cols), cols)]


def cut_columns(x, mates):
    rows, width = x.shape
    count = mates.shape[0]
    whole = pl.BlockSpec(memory_space=pltpu.VMEM)
    shape = jax.ShapeDtypeStruct((rows, width // count), x.dtype)
    return pl.pallas_call(
        cut_kernel,
        in_specs=[pl.BlockSpec(memory_space=pltpu.SMEM), whole],
        out_specs=[whole] * count,
        out_shape=[shape] * count,
    )(mates, x)


def lay_kernel(mates_ref, *refs):
    *blocks, out_ref = refs
    cols = blocks[0].shape[1]
    for j, ref in enumerate(blocks):
        out_ref[:, pl.ds(pl.multiple_of(mates_ref[j] * cols, cols), cols)] = ref[...]


def lay_columns(blocks, mates):
    rows, cols = blocks[0].shape
    whole = pl.BlockSpec(memory_space=pltpu.VMEM)
    return pl.pallas_call(
        lay_kernel,
        in_specs=[pl.BlockSpec(memory_space=pltpu.SMEM)] + [whole] * len(blocks),
        out_specs=whole,
        out_shape=jax.ShapeDtypeStruct((rows, cols * len(blocks)), blocks[0].dtype),
    )(mates, *blocks)


def state_kernel(dim, place_ref, k_ref, v_ref, cum_ref, out_ref):
    cum = cum_ref[...]
    fade = jnp.exp(cum[-1:, :] - cum)
    for h in range(cum.shape[1]):
        lanes = slice(h * dim, (h + 1) * dim)
        faded = (k_ref[0, :, lanes].astype(F32) * fade[:, h : h + 1]).astype(BF)
        out_ref[0, h] = lax.dot_general(
            faded, v_ref[0, :, lanes], (((0,), (0,)), ((), ())), preferred_element_type=F32
        ).astype(BF)


def local_states(keys, values, cum, place, first, seqs):
    _, block, width = keys.shape
    heads = cum.shape[1]
    dim = width // 2 // heads
    rows = pl.BlockSpec((1, block, width // 2), lambda s, place: (s + first, 0, place[0]))
    return pl.pallas_call(
        functools.partial(state_kernel, dim),
        grid_spec=pltpu.PrefetchScalarGridSpec(
            num_scalar_prefetch=1,
            grid=(seqs,),
            in_specs=[rows, rows, pl.BlockSpec((block, heads), lambda s, place: (0, 0))],
            out_specs=pl.BlockSpec((1, heads, dim, dim), lambda s, place: (s, 0, 0, 0)),
        ),
        out_shape=jax.ShapeDtypeStruct((seqs, heads, dim, dim), BF),
        compiler_params=pltpu.CompilerParams(vmem_limit_bytes=60 * MIB),
        cost_estimate=pl.CostEstimate(
            flops=2000000000, bytes_accessed=2 * seqs * width * (block + dim), transcendentals=0
        ),
    )(place.reshape(1).astype(jnp.int32), keys, values, cum)


def within_kernel(dim, q_ref, k_ref, v_ref, g_ref, cum_ref, cumt_ref, gain_ref, out_ref, act_ref):
    cum = cum_ref[...]
    block = cum.shape[0]
    causal = lax.broadcasted_iota(jnp.int32, (block, block), 0) >= lax.broadcasted_iota(
        jnp.int32, (block, block), 1
    )
    for h in range(cum.shape[1]):
        lanes = slice(h * dim, (h + 1) * dim)
        scores = lax.dot_general(
            q_ref[0, :, lanes],
            k_ref[0, :, lanes],
            (((1,), (1,)), ((), ())),
            preferred_element_type=F32,
        )
        gap = jnp.where(causal, cum[:, h : h + 1] - cumt_ref[h : h + 1, :], -1e30)
        weights = (scores * jnp.exp(gap)).astype(BF)
        out_ref[0, :, lanes] = jnp.dot(weights, v_ref[0, :, lanes], preferred_element_type=F32)
    act_ref[0] = gain_ref[...] * jax.nn.sigmoid(g_ref[0].astype(F32))


def within_block(queries, keys, values, gate, cum, head_gain, first, seqs):
    _, block, width = keys.shape
    heads = cum.shape[1]
    dim = width // heads
    rows = pl.BlockSpec((1, block, width), lambda s: (s + first, 0, 0))
    out = pl.BlockSpec((1, block, width), lambda s: (s, 0, 0))
    shape = jax.ShapeDtypeStruct((seqs, block, width), F32)
    return pl.pallas_call(
        functools.partial(within_kernel, dim),
        grid=(seqs,),
        in_specs=[
            rows,
            rows,
            rows,
            rows,
            pl.BlockSpec((block, heads), lambda s: (0, 0)),
            pl.BlockSpec((heads, block), lambda s: (0, 0)),
            pl.BlockSpec((1, width), lambda s: (0, 0)),
        ],
        out_specs=[out, out],
        out_shape=[shape, shape],
        compiler_params=pltpu.CompilerParams(vmem_limit_bytes=60 * MIB),
        cost_estimate=pl.CostEstimate(
            flops=60 * seqs * block * block * width,
            bytes_accessed=16 * seqs * block * width,
            transcendentals=seqs * block * width,
        ),
    )(queries, keys, values, gate, cum, cum.T, head_gain[None])


def combine_kernel(weight_ref, *refs):
    *states, out_ref = refs
    for h in range(out_ref.shape[1]):
        out_ref[0, h] = sum(
            weight_ref[i, h] * ref[0, h].astype(F32) for i, ref in enumerate(states)
        ).astype(BF)


def combine(states, weights):
    seqs, heads, dim, _ = states[0].shape
    block = pl.BlockSpec((1, heads, dim, dim), lambda s: (s, 0, 0, 0))
    return pl.pallas_call(
        combine_kernel,
        grid=(seqs,),
        in_specs=[pl.BlockSpec(memory_space=pltpu.SMEM)] + [block] * len(states),
        out_specs=block,
        out_shape=jax.ShapeDtypeStruct(states[0].shape, BF),
        compiler_params=pltpu.CompilerParams(vmem_limit_bytes=16 * MIB),
    )(weights, *states)


def mixed_kernel(
    dim, sub, side_ref, weight_ref, q_ref, own_ref, got_ref, pair_own_ref, pair_got_ref,
    within_ref, act_ref, cum_ref, out_ref,
):
    scale = jnp.exp(cum_ref[...])
    heads = scale.shape[1]
    half = heads // 2
    for h in range(heads):
        lanes = slice(h * dim, (h + 1) * dim)
        here = side_ref[0] == h // half
        entering = jnp.where(here, own_ref[0, h % half], got_ref[0, h % half]).astype(F32)
        paired = jnp.where(here, pair_own_ref[0, h % half], pair_got_ref[0, h % half]).astype(F32)
        state = (weight_ref[0, h] * entering + weight_ref[1, h] * paired).astype(BF)
        carried = jnp.dot(q_ref[0, :, lanes], state, preferred_element_type=F32)
        attended = within_ref[0, :, lanes] + carried * scale[:, h : h + 1]
        square = jnp.mean(attended * attended, axis=1, keepdims=True)
        mixed = (attended * lax.rsqrt(square + 1e-06) * act_ref[0, :, lanes]).astype(BF)
        for d in range(out_ref.shape[0]):
            out_ref[d, 0, :, lanes] = mixed[d * sub : (d + 1) * sub]


def mixed_rows(queries, states, weights, side, within, act, cum, sub, first, seqs):
    _, block, width = queries.shape
    heads = cum.shape[1]
    dim = width // heads
    parts = block // sub
    rows = pl.BlockSpec((1, block, width), lambda s, side: (s + first, 0, 0))
    here = pl.BlockSpec((1, block, width), lambda s, side: (s, 0, 0))
    halved = pl.BlockSpec((1, heads // 2, dim, dim), lambda s, side: (s, 0, 0, 0))
    return pl.pallas_call(
        functools.partial(mixed_kernel, dim, sub),
        grid_spec=pltpu.PrefetchScalarGridSpec(
            num_scalar_prefetch=1,
            grid=(seqs,),
            in_specs=[pl.BlockSpec(memory_space=pltpu.SMEM), rows]
            + [halved] * 4
            + [here, here, pl.BlockSpec((block, heads), lambda s, side: (0, 0))],
            out_specs=pl.BlockSpec((parts, 1, sub, width), lambda s, side: (0, s, 0, 0)),
        ),
        out_shape=jax.ShapeDtypeStruct((parts, seqs, sub, width), BF),
        compiler_params=pltpu.CompilerParams(vmem_limit_bytes=60 * MIB),
        cost_estimate=pl.CostEstimate(
            flops=6000000000, bytes_accessed=14 * seqs * block * width, transcendentals=0
        ),
    )(side.reshape(1).astype(jnp.int32), weights, queries, *states, within, act, cum)


def project_kernel(sizes, order_ref, *refs):
    *pieces, w_ref, out_ref = refs
    parts, _, rows, _ = out_ref.shape
    at = 0
    for ref, size in zip(pieces, sizes):
        for i in range(size):
            product = jnp.dot(ref[i], w_ref[...], preferred_element_type=F32).astype(BF)
            for d in range(parts):
                out_ref[d, order_ref[at]] = product[d * rows : (d + 1) * rows]
            at += 1


def project(pieces, weight, order, parts):
    count = sum(p.shape[0] for p in pieces)
    rows, depth = pieces[0].shape[1:]
    cols = weight.shape[1]
    whole = pl.BlockSpec(memory_space=pltpu.VMEM)
    return pl.pallas_call(
        functools.partial(project_kernel, [p.shape[0] for p in pieces]),
        in_specs=[pl.BlockSpec(memory_space=pltpu.SMEM)] + [whole] * (len(pieces) + 1),
        out_specs=whole,
        out_shape=jax.ShapeDtypeStruct((parts, count, rows // parts, cols), BF),
        compiler_params=pltpu.CompilerParams(vmem_limit_bytes=20 * MIB),
        cost_estimate=pl.CostEstimate(
            flops=4 * count * rows * depth * cols,
            bytes_accessed=2 * (count * rows * (depth + cols) + depth * cols),
            transcendentals=0,
        ),
    )(order, *pieces, weight)


def residual_kernel(count, mates_ref, *refs):
    stream, sums = refs[:count], refs[count:-2]
    out_ref, square_ref = refs[-2:]
    rows = out_ref.shape[1] // len(sums)
    for j in range(count):
        out_ref[mates_ref[j]] = stream[j][...].astype(F32)
    for b in range(count):
        for h, ref in enumerate(sums):
            at = slice(h * rows, (h + 1) * rows)
            total = out_ref[b, at] + ref[b].astype(F32)
            out_ref[b, at] = total
            square_ref[b, at] = jnp.sum(total * total, axis=1, keepdims=True)


def residual_sums(mates, stream, sums):
    count = len(stream)
    rows, cols = stream[0].shape
    whole = pl.BlockSpec(memory_space=pltpu.VMEM)
    return pl.pallas_call(
        functools.partial(residual_kernel, count),
        in_specs=[pl.BlockSpec(memory_space=pltpu.SMEM)] + [whole] * (count + len(sums)),
        out_specs=[whole] * 2,
        out_shape=[
            jax.ShapeDtypeStruct((count, rows, cols), F32),
            jax.ShapeDtypeStruct((count, rows, 1), F32),
        ],
        compiler_params=pltpu.CompilerParams(vmem_limit_bytes=32 * MIB),
    )(mates, *stream, *sums)


def hidden_kernel(sizes, groups, order_ref, *refs):
    steps = sum(sizes)
    each = len(sizes)
    pieces = [refs[g * each : (g + 1) * each] for g in range(groups)]
    refs = refs[groups * each :]
    (gate_ref, up_ref), outs = refs[:2], refs[2:]
    outs, g_acc, u_acc = outs[:groups], outs[-2], outs[-1]
    i = pl.program_id(0)
    hid = gate_ref.shape[1]
    main = hid - 128 if hid % 256 == 128 else hid

    def products(rows):
        for acc, ref in ((g_acc, gate_ref), (u_acc, up_ref)):
            yield acc, slice(0, main), jnp.dot(rows, ref[:, :main], preferred_element_type=F32)
        if main < hid:
            rest = jnp.concatenate([gate_ref[:, main:], up_ref[:, main:]], axis=1)
            both = jnp.dot(rows, rest, preferred_element_type=F32)
            yield g_acc, slice(main, hid), both[:, : hid - main]
            yield u_acc, slice(main, hid), both[:, hid - main :]

    start = 0
    for p, size in enumerate(sizes):

        @pl.when((i >= start) & (i < start + size))
        def _(p=p, start=start):
            for g in range(groups):
                rows = pieces[g][p][0]
                for acc, at, product in products(rows):
                    if start == 0:
                        acc[g, :, at] = product
                    else:
                        acc[g, :, at] += product

        start += size

    @pl.when(i == steps - 1)
    def _():
        for g in range(groups):
            v = g_acc[g]
            outs[g][...] = (v / (1.0 + jnp.exp(-v)) * u_acc[g]).astype(BF)


def hidden_units(groups, w_gate, w_up, order):
    sizes = [p.shape[0] for p in groups[0]]
    rows, cols = groups[0][0].shape[1:]
    depth, hid = w_gate.shape
    many = len(groups)
    specs = []
    start = 0
    for size in sizes:
        specs.append(
            pl.BlockSpec(
                (1, rows, cols),
                lambda i, order, start=start, size=size: (jnp.clip(i - start, 0, size - 1), 0, 0),
            )
        )
        start += size
    up_spec = pl.BlockSpec((cols, hid), lambda i, order: (order[i], 0))
    return pl.pallas_call(
        functools.partial(hidden_kernel, sizes, many),
        grid_spec=pltpu.PrefetchScalarGridSpec(
            num_scalar_prefetch=1,
            grid=(sum(sizes),),
            in_specs=specs * many
            + [up_spec, up_spec],
            out_specs=[pl.BlockSpec((rows, hid), lambda i, order: (0, 0))] * many,
            scratch_shapes=[pltpu.VMEM((many, rows, hid), F32)] * 2,
        ),
        out_shape=[jax.ShapeDtypeStruct((rows, hid), BF)] * many,
        compiler_params=pltpu.CompilerParams(vmem_limit_bytes=60 * MIB),
        cost_estimate=pl.CostEstimate(
            flops=8 * many * rows * depth * hid,
            bytes_accessed=4 * depth * hid + 2 * many * rows * depth,
            transcendentals=many * rows * hid,
        ),
    )(order, *[p for pieces in groups for p in pieces], w_gate, w_up)


def down_kernel(groups, order_ref, *refs):
    hidden, weight, outs = refs[:groups], refs[groups], refs[groups + 1 :]
    for g in range(groups):
        outs[g][0] = jnp.dot(hidden[g][...], weight[...], preferred_element_type=F32).astype(BF)


def down_blocks(hidden, w_down, order):
    many = len(hidden)
    rows, hid = hidden[0].shape
    blocks, model = order.shape[0], w_down.shape[1]
    cols = model // lax.axis_size("ctx")

    return pl.pallas_call(
        functools.partial(down_kernel, many),
        grid_spec=pltpu.PrefetchScalarGridSpec(
            num_scalar_prefetch=1,
            grid=(blocks,),
            in_specs=[pl.BlockSpec((rows, hid), lambda i, order: (0, 0))] * many
            + [pl.BlockSpec((hid, cols), lambda i, order: (0, order[i]))],
            out_specs=[pl.BlockSpec((1, rows, cols), lambda i, order: (i, 0, 0))] * many,
        ),
        out_shape=[jax.ShapeDtypeStruct((blocks, rows, cols), BF)] * many,
        compiler_params=pltpu.CompilerParams(vmem_limit_bytes=60 * MIB),
        cost_estimate=pl.CostEstimate(
            flops=4 * many * rows * cols * blocks * hid,
            bytes_accessed=2 * cols * blocks * hid + 2 * many * rows * cols * blocks,
            transcendentals=0,
        ),
    )(order, *hidden, w_down)


def body(
    queries,
    keys,
    values,
    decay_log,
    out_gate,
    head_gain,
    out_weight,
    stream,
    norm_gain,
    expert_ids,
    expert_share,
    w_gate,
    w_up,
    w_down,
):
    count = lax.axis_size("ctx")
    parts = lax.axis_size("exp")
    me = lax.axis_index("ctx")
    mine = lax.axis_index("exp")
    side = me & 1
    seqs, block, width = queries.shape
    heads = decay_log.shape[1]
    sub, model = stream.shape[1:]
    tokens = seqs * sub
    cols = model // count
    order = block_order(count, me)
    order_array = jnp.stack(order).astype(jnp.int32)

    cum = jnp.cumsum(decay_log, axis=0)
    small = jnp.concatenate(
        [
            expert_ids.reshape(2 * tokens).astype(F32),
            expert_share.reshape(2 * tokens),
            cum[-1],
        ]
    )
    cum_mine = lax.dynamic_slice_in_dim(cum, side * (heads // 2), heads // 2, 1)
    cum_theirs = lax.dynamic_slice_in_dim(cum, (1 - side) * (heads // 2), heads // 2, 1)
    halves = 2
    each = seqs // halves
    state_theirs = local_states(keys, values, cum_theirs, 1 - side, 0, each)
    small = jnp.pad(small, (0, -small.shape[0] % 128)).reshape(-1, 128)
    facts = joined(spread(after(small, state_theirs), count)).reshape(count, -1)
    steps = len(routes(count)[0])
    place = order_array[None, :] == jnp.arange(count, dtype=jnp.int32)[:, None]
    facts = jnp.sum(jnp.where(place[:, :, None], facts[None], 0.0), axis=1)
    ids = facts[:, : 2 * tokens].astype(jnp.int32)
    shares = facts[:, 2 * tokens : 4 * tokens]
    ends = facts[:, 4 * tokens : 4 * tokens + heads]

    mates = (me ^ jnp.arange(count, dtype=jnp.int32)).astype(jnp.int32)

    block_no = jnp.arange(count)

    def faded(source, target):
        between = (block_no >= 2 * (source // 2 + 1)) & (block_no < 2 * (target // 2))
        power = jnp.sum(jnp.where(between[:, None], ends, 0.0), axis=0)
        return jnp.where(source // 2 < target // 2, jnp.exp(power), 0.0)

    half_heads = heads // 2

    def side_half(row):
        return lax.dynamic_slice_in_dim(row, side * half_heads, half_heads, 0)

    fade_own = jnp.exp(cum[-1])
    lanes = jnp.pad(cum[-1:], ((0, 0), (0, -heads % 128)))
    fade_other = jnp.exp(send(lanes, pair(count))[0, :heads])
    ones = jnp.ones_like(fade_own)
    chip_weights = jnp.stack(
        [
            side_half(jnp.where(side == 0, fade_other, ones)),
            side_half(jnp.where(side == 0, ones, fade_own)),
        ]
    )
    enter_weights = jnp.stack(
        [jnp.where(side == 0, ones, fade_other), jnp.where(side == 0, 0.0, ones)]
    )

    there = me ^ hop_mask(count, steps - 1, side)
    summed = []
    arrivals, mixed, spreads = (), None, ()
    for h in range(halves):
        first = h * each
        if h:
            state_theirs = local_states(
                keys, values, after(cum_theirs, *arrivals[:1]), 1 - side, first, each
            )
        state_mine = local_states(
            keys, values, after(cum_mine, *arrivals[:1]), side, first, each
        )
        other_mine = send(state_theirs, pair(count))
        other_theirs = send(state_mine, pair(count))
        chip = combine([state_mine, other_mine], chip_weights)
        within, act = within_block(
            queries,
            keys,
            values,
            out_gate,
            after(cum, chip if mixed is None else mixed),
            head_gain,
            first,
            each,
        )
        held, names = [after(chip, *arrivals[1:])], [me]
        for step in range(steps - 1):
            got = send(jnp.stack(held) if step else held[0][None], hop(count, step))
            mask = hop_mask(count, step, side)
            held = held + [got[i] for i in range(len(held))]
            names = names + [name ^ mask for name in names]
        towards = [jnp.stack([side_half(faded(name, t)) for name in names]) for t in (there, me)]
        leaving = combine(held, after(towards[0], within, *spreads[1:2]))
        got = send(leaving, hop(count, steps - 1))
        arrivals = (held[-1], got)
        alone = jnp.concatenate([towards[1], jnp.ones((1, half_heads), F32)])
        entering = combine(held + [got], alone)
        states = [entering, send(entering, pair(count)), other_mine, other_theirs]
        mixed = mixed_rows(
            queries, states, enter_weights, side, within, act, cum, sub, first, each
        )
        gates = [spreads[2:3]] + [()] * (steps - 1) + [(partial,)] if h else ()
        pieces = spread(mixed.reshape(parts * each * sub, width), count, gates)
        partial = project(pieces, out_weight, order_array, parts)
        spreads = tuple(pieces)
        summed.append(lax.psum_scatter(partial, "exp", scatter_dimension=0))

    stream_rows = after(stream, partial).reshape(tokens, model)
    stream_got = swap_blocks(cut_columns(stream_rows, mates), count)
    residual, square = residual_sums(mates, stream_got, summed)
    residual = residual.reshape(count * tokens, cols)

    square = sum_over(square.reshape(count * tokens), count)
    scale = lax.rsqrt(square / model + 1e-06)
    gain = lax.dynamic_slice_in_dim(norm_gain, me * cols, cols, 0)
    rows_in = (residual * scale[:, None] * gain).astype(BF)

    expert_local = w_gate.shape[0]
    experts = expert_local * parts
    capacity = max(2, (2 * tokens + experts - 1) // experts + 1)
    one_hot = ids[:, :, None] == jnp.arange(experts, dtype=jnp.int32)
    earlier = jnp.arange(2 * tokens)[:, None] > jnp.arange(2 * tokens)[None, :]
    ahead = jnp.einsum(
        "tu,gue->gte", earlier.astype(BF), one_hot.astype(BF), preferred_element_type=F32
    )
    ranking = jnp.sum(jnp.where(one_hot, ahead, 0.0), axis=2).astype(jnp.int32)
    slots = capacity * count
    turned = (ids - mine + experts) % experts
    slot_of = (turned * count + jnp.arange(count, dtype=jnp.int32)[:, None]) * capacity + ranking
    slot_of = slot_of.reshape(count * tokens, 2)
    share_of = shares.reshape(count * tokens, 2)
    turns = [*range(0, parts, 2), *range(1, parts, 2)]
    sent = []
    for turn in turns:
        numbers = turn * slots + jnp.arange(slots, dtype=jnp.int32)
        hit = [slot_of[:, k][None, :] == numbers[:, None] for k in range(2)]
        placing = hit[0] | hit[1]
        dispatch = jnp.dot(placing.astype(BF), rows_in, preferred_element_type=F32).astype(BF)
        if turn:
            dispatch = lax.ppermute(dispatch, "exp", [(i, (i + turn) % parts) for i in range(parts)])
        sent.append(dispatch)

    arrived = []
    for turn in range(parts):
        gates = [()] * steps
        if turn == 0:
            gates[-1] = (sent[1],)
        elif turn == 1:
            gates[-1] = (arrived[0][steps], sent[2 % parts])
            gates.append((sent[3 % parts],))
        else:
            gates[0] = (arrived[0 if turn < 4 else turn - 2][steps],)
        arrived.append(spread(sent[turn], count, gates))
    near_order, far_order = order_array[: count // 2], order_array[count // 2 :]
    returned = []
    waits, moved = [], [[]] * steps
    for first in range(0, parts, 2):
        now = range(first, min(first + 2, parts))
        later = range(first + 2, min(first + 4, parts))
        ready = [arrived[t][1] for t in later]
        groups = [arrived[t] for t in now]
        groups[0] = list(after(tuple(groups[0]), *waits, *ready))
        hidden = hidden_units(groups, w_gate[0], w_up[0], order_array)
        ready = [arrived[t][steps] for t in later]
        far = down_blocks(after(tuple(hidden), *ready, *moved[0]), w_down[0], far_order)
        ready = [arrived[t][-1] for t in later]
        near = down_blocks(after(tuple(hidden), *far, *ready), w_down[0], near_order)
        totals = [pair_sum(n, f, count) for n, f in zip(near, far)]
        waits = [leaves for _, leaves in totals]
        before = tuple(moved[-1])
        moved = [[] for _ in range(steps)]
        for turn, total in zip(turns[first : first + 2], totals):
            done, got = gathered_sum(total, count, (before,))
            for step in range(steps):
                moved[step].append(got[step])
            if first + 2 >= parts:
                before = (got[0],)
            if turn:
                back = [((i + turn) % parts, i) for i in range(parts)]
                done = lax.ppermute(done, "exp", back)
            returned.append(done)
    result = residual
    for at, turn in enumerate(turns):
        numbers = turn * slots + jnp.arange(slots, dtype=jnp.int32)
        weighting = sum(
            jnp.where(slot_of[:, k][:, None] == numbers[None, :], share_of[:, k][:, None], 0.0)
            for k in range(2)
        )
        high = weighting.astype(BF)
        low = (weighting - high.astype(F32)).astype(BF)
        result = result + jnp.dot(high, returned[at], preferred_element_type=F32)
        result = result + jnp.dot(low, returned[at], preferred_element_type=F32)
    result = result.astype(BF).reshape(count, tokens, cols)
    blocks = [lax.dynamic_index_in_dim(result, me ^ j, 0, False) for j in range(count)]
    return lay_columns(swap_blocks(blocks, count), mates).reshape(seqs, sub, model)


def solution(mesh):
    return jax.shard_map(
        body,
        mesh=mesh,
        in_specs=(
            P(None, "ctx", "exp"),
            P(None, "ctx", "exp"),
            P(None, "ctx", "exp"),
            P("ctx", "exp"),
            P(None, "ctx", "exp"),
            P("exp"),
            P("exp", "ctx"),
            P(None, ("ctx", "exp"), None),
            P(),
            P(("ctx", "exp"), None, None),
            P(("ctx", "exp"), None, None),
            P("exp", None, "ctx"),
            P("exp", None, "ctx"),
            P("exp", "ctx", None),
        ),
        out_specs=P(None, ("ctx", "exp"), None),
        check_vma=False,
    )
```

```python
import functools

import jax
import jax.numpy as jnp
from jax import lax
from jax.experimental import pallas as pl
from jax.experimental.pallas import tpu as pltpu
from jax.sharding import PartitionSpec as P

MIB = 1 << 20
BF = jnp.bfloat16
F32 = jnp.float32


def routes(count):
    bits = [1 << b for b in range(1, count.bit_length() - 1)]
    turn = len(bits) // 2
    return bits, bits[turn:] + bits[:turn]


def hop(count, step):
    both = routes(count)
    return [(i, i ^ both[i & 1][step]) for i in range(count)]


def hop_mask(count, step, side):
    both = routes(count)
    return jnp.where(side == 0, both[0][step], both[1][step])


def pair(count):
    return [(i, i ^ 1) for i in range(count)]


def held_by(count, who):
    held = [who]
    for step in range(len(routes(count)[0])):
        mask = hop_mask(count, step, who & 1)
        held = held + [h ^ mask for h in held]
    return held


def block_order(count, me):
    return held_by(count, me) + held_by(count, me ^ 1)


def send(x, perm):
    return lax.ppermute(x, "ctx", perm)


def after(x, *others):
    return lax.optimization_barrier((x, *others))[0]


def joined(parts):
    return parts[0] if len(parts) == 1 else jnp.concatenate(parts, axis=0)


def spread(x, count, gates=()):
    pieces = [x[None]]
    for step in range(len(routes(count)[0])):
        block = joined(pieces)
        if step < len(gates):
            block = after(block, *gates[step])
        pieces.append(send(block, hop(count, step)))
    block = tuple(pieces)
    if len(gates) > len(routes(count)[0]):
        block = after(block, *gates[-1])
    return pieces + [send(x, pair(count)) for x in block]


def halved_sum(x, other):
    half = max(1, x.shape[0] // 2)

    def added(at):
        return (x[at].astype(F32) + other[at].astype(F32)).astype(BF)

    if x.shape[0] == 1:
        return added(slice(0, 1)), None
    return added(slice(0, half)), added(slice(half, None))


def pair_sum(near, far, count):
    return halved_sum(near, send(far, pair(count)))


def gathered_sum(total, count, gates=()):
    got = []
    stays, leaves = total
    for at, step in enumerate(reversed(range(len(routes(count)[0])))):
        if at < len(gates):
            leaves = after(leaves, *gates[at])
        got.append(send(leaves, hop(count, step)))
        stays, leaves = halved_sum(stays, got[-1])
    return stays[0], got


def sum_over(x, count):
    for bit in range(count.bit_length() - 1):
        x = x + send(x, [(i, i ^ (1 << bit)) for i in range(count)])
    return x


def swap_blocks(blocks, count):
    got = [blocks[0]]
    for j in range(1, count):
        got.append(send(blocks[j], [(i, i ^ j) for i in range(count)]))
    return got


def cut_kernel(mates_ref, x_ref, *outs):
    cols = outs[0].shape[1]
    for j, out in enumerate(outs):
        out[...] = x_ref[:, pl.ds(pl.multiple_of(mates_ref[j] * cols, cols), cols)]


def cut_columns(x, mates):
    rows, width = x.shape
    count = mates.shape[0]
    whole = pl.BlockSpec(memory_space=pltpu.VMEM)
    shape = jax.ShapeDtypeStruct((rows, width // count), x.dtype)
    return pl.pallas_call(
        cut_kernel,
        in_specs=[pl.BlockSpec(memory_space=pltpu.SMEM), whole],
        out_specs=[whole] * count,
        out_shape=[shape] * count,
    )(mates, x)


def lay_kernel(mates_ref, *refs):
    *blocks, out_ref = refs
    cols = blocks[0].shape[1]
    for j, ref in enumerate(blocks):
        out_ref[:, pl.ds(pl.multiple_of(mates_ref[j] * cols, cols), cols)] = ref[...]


def lay_columns(blocks, mates):
    rows, cols = blocks[0].shape
    whole = pl.BlockSpec(memory_space=pltpu.VMEM)
    return pl.pallas_call(
        lay_kernel,
        in_specs=[pl.BlockSpec(memory_space=pltpu.SMEM)] + [whole] * len(blocks),
        out_specs=whole,
        out_shape=jax.ShapeDtypeStruct((rows, cols * len(blocks)), blocks[0].dtype),
    )(mates, *blocks)


def state_kernel(dim, place_ref, k_ref, v_ref, cum_ref, out_ref):
    cum = cum_ref[...]
    fade = jnp.exp(cum[-1:, :] - cum)
    for h in range(cum.shape[1]):
        lanes = slice(h * dim, (h + 1) * dim)
        faded = (k_ref[0, :, lanes].astype(F32) * fade[:, h : h + 1]).astype(BF)
        out_ref[0, h] = lax.dot_general(
            faded, v_ref[0, :, lanes], (((0,), (0,)), ((), ())), preferred_element_type=F32
        ).astype(BF)


def local_states(keys, values, cum, place, first, seqs):
    _, block, width = keys.shape
    heads = cum.shape[1]
    dim = width // 2 // heads
    rows = pl.BlockSpec((1, block, width // 2), lambda s, place: (s + first, 0, place[0]))
    return pl.pallas_call(
        functools.partial(state_kernel, dim),
        grid_spec=pltpu.PrefetchScalarGridSpec(
            num_scalar_prefetch=1,
            grid=(seqs,),
            in_specs=[rows, rows, pl.BlockSpec((block, heads), lambda s, place: (0, 0))],
            out_specs=pl.BlockSpec((1, heads, dim, dim), lambda s, place: (s, 0, 0, 0)),
        ),
        out_shape=jax.ShapeDtypeStruct((seqs, heads, dim, dim), BF),
        compiler_params=pltpu.CompilerParams(vmem_limit_bytes=60 * MIB),
        cost_estimate=pl.CostEstimate(
            flops=2000000000, bytes_accessed=2 * seqs * width * (block + dim), transcendentals=0
        ),
    )(place.reshape(1).astype(jnp.int32), keys, values, cum)


def within_kernel(dim, q_ref, k_ref, v_ref, g_ref, cum_ref, cumt_ref, gain_ref, out_ref, act_ref):
    cum = cum_ref[...]
    block = cum.shape[0]
    causal = lax.broadcasted_iota(jnp.int32, (block, block), 0) >= lax.broadcasted_iota(
        jnp.int32, (block, block), 1
    )
    for h in range(cum.shape[1]):
        lanes = slice(h * dim, (h + 1) * dim)
        scores = lax.dot_general(
            q_ref[0, :, lanes],
            k_ref[0, :, lanes],
            (((1,), (1,)), ((), ())),
            preferred_element_type=F32,
        )
        gap = jnp.where(causal, cum[:, h : h + 1] - cumt_ref[h : h + 1, :], -1e30)
        weights = (scores * jnp.exp(gap)).astype(BF)
        out_ref[0, :, lanes] = jnp.dot(weights, v_ref[0, :, lanes], preferred_element_type=F32)
    act_ref[0] = gain_ref[...] * jax.nn.sigmoid(g_ref[0].astype(F32))


def within_block(queries, keys, values, gate, cum, head_gain, first, seqs):
    _, block, width = keys.shape
    heads = cum.shape[1]
    dim = width // heads
    rows = pl.BlockSpec((1, block, width), lambda s: (s + first, 0, 0))
    out = pl.BlockSpec((1, block, width), lambda s: (s, 0, 0))
    shape = jax.ShapeDtypeStruct((seqs, block, width), F32)
    return pl.pallas_call(
        functools.partial(within_kernel, dim),
        grid=(seqs,),
        in_specs=[
            rows,
            rows,
            rows,
            rows,
            pl.BlockSpec((block, heads), lambda s: (0, 0)),
            pl.BlockSpec((heads, block), lambda s: (0, 0)),
            pl.BlockSpec((1, width), lambda s: (0, 0)),
        ],
        out_specs=[out, out],
        out_shape=[shape, shape],
        compiler_params=pltpu.CompilerParams(vmem_limit_bytes=60 * MIB),
        cost_estimate=pl.CostEstimate(
            flops=60 * seqs * block * block * width,
            bytes_accessed=16 * seqs * block * width,
            transcendentals=seqs * block * width,
        ),
    )(queries, keys, values, gate, cum, cum.T, head_gain[None])


def combine_kernel(weight_ref, *refs):
    *states, out_ref = refs
    for h in range(out_ref.shape[1]):
        out_ref[0, h] = sum(
            weight_ref[i, h] * ref[0, h].astype(F32) for i, ref in enumerate(states)
        ).astype(BF)


def combine(states, weights):
    seqs, heads, dim, _ = states[0].shape
    block = pl.BlockSpec((1, heads, dim, dim), lambda s: (s, 0, 0, 0))
    return pl.pallas_call(
        combine_kernel,
        grid=(seqs,),
        in_specs=[pl.BlockSpec(memory_space=pltpu.SMEM)] + [block] * len(states),
        out_specs=block,
        out_shape=jax.ShapeDtypeStruct(states[0].shape, BF),
        compiler_params=pltpu.CompilerParams(vmem_limit_bytes=16 * MIB),
    )(weights, *states)


def mixed_kernel(
    dim, sub, side_ref, weight_ref, q_ref, own_ref, got_ref, pair_own_ref, pair_got_ref,
    within_ref, act_ref, cum_ref, out_ref,
):
    scale = jnp.exp(cum_ref[...])
    heads = scale.shape[1]
    half = heads // 2
    for h in range(heads):
        lanes = slice(h * dim, (h + 1) * dim)
        here = side_ref[0] == h // half
        entering = jnp.where(here, own_ref[0, h % half], got_ref[0, h % half]).astype(F32)
        paired = jnp.where(here, pair_own_ref[0, h % half], pair_got_ref[0, h % half]).astype(F32)
        state = (weight_ref[0, h] * entering + weight_ref[1, h] * paired).astype(BF)
        carried = jnp.dot(q_ref[0, :, lanes], state, preferred_element_type=F32)
        attended = within_ref[0, :, lanes] + carried * scale[:, h : h + 1]
        square = jnp.mean(attended * attended, axis=1, keepdims=True)
        mixed = (attended * lax.rsqrt(square + 1e-06) * act_ref[0, :, lanes]).astype(BF)
        for d in range(out_ref.shape[0]):
            out_ref[d, 0, :, lanes] = mixed[d * sub : (d + 1) * sub]


def mixed_rows(queries, states, weights, side, within, act, cum, sub, first, seqs):
    _, block, width = queries.shape
    heads = cum.shape[1]
    dim = width // heads
    parts = block // sub
    rows = pl.BlockSpec((1, block, width), lambda s, side: (s + first, 0, 0))
    here = pl.BlockSpec((1, block, width), lambda s, side: (s, 0, 0))
    halved = pl.BlockSpec((1, heads // 2, dim, dim), lambda s, side: (s, 0, 0, 0))
    return pl.pallas_call(
        functools.partial(mixed_kernel, dim, sub),
        grid_spec=pltpu.PrefetchScalarGridSpec(
            num_scalar_prefetch=1,
            grid=(seqs,),
            in_specs=[pl.BlockSpec(memory_space=pltpu.SMEM), rows]
            + [halved] * 4
            + [here, here, pl.BlockSpec((block, heads), lambda s, side: (0, 0))],
            out_specs=pl.BlockSpec((parts, 1, sub, width), lambda s, side: (0, s, 0, 0)),
        ),
        out_shape=jax.ShapeDtypeStruct((parts, seqs, sub, width), BF),
        compiler_params=pltpu.CompilerParams(vmem_limit_bytes=60 * MIB),
        cost_estimate=pl.CostEstimate(
            flops=6000000000, bytes_accessed=14 * seqs * block * width, transcendentals=0
        ),
    )(side.reshape(1).astype(jnp.int32), weights, queries, *states, within, act, cum)


def project_kernel(sizes, order_ref, *refs):
    *pieces, w_ref, out_ref = refs
    parts, _, rows, _ = out_ref.shape
    at = 0
    for ref, size in zip(pieces, sizes):
        for i in range(size):
            product = jnp.dot(ref[i], w_ref[...], preferred_element_type=F32).astype(BF)
            for d in range(parts):
                out_ref[d, order_ref[at]] = product[d * rows : (d + 1) * rows]
            at += 1


def project(pieces, weight, order, parts):
    count = sum(p.shape[0] for p in pieces)
    rows, depth = pieces[0].shape[1:]
    cols = weight.shape[1]
    whole = pl.BlockSpec(memory_space=pltpu.VMEM)
    return pl.pallas_call(
        functools.partial(project_kernel, [p.shape[0] for p in pieces]),
        in_specs=[pl.BlockSpec(memory_space=pltpu.SMEM)] + [whole] * (len(pieces) + 1),
        out_specs=whole,
        out_shape=jax.ShapeDtypeStruct((parts, count, rows // parts, cols), BF),
        compiler_params=pltpu.CompilerParams(vmem_limit_bytes=20 * MIB),
        cost_estimate=pl.CostEstimate(
            flops=4 * count * rows * depth * cols,
            bytes_accessed=2 * (count * rows * (depth + cols) + depth * cols),
            transcendentals=0,
        ),
    )(order, *pieces, weight)


def residual_kernel(count, mates_ref, *refs):
    stream, sums = refs[:count], refs[count:-2]
    out_ref, square_ref = refs[-2:]
    rows = out_ref.shape[1] // len(sums)
    for j in range(count):
        out_ref[mates_ref[j]] = stream[j][...].astype(F32)
    for b in range(count):
        for h, ref in enumerate(sums):
            at = slice(h * rows, (h + 1) * rows)
            total = out_ref[b, at] + ref[b].astype(F32)
            out_ref[b, at] = total
            square_ref[b, at] = jnp.sum(total * total, axis=1, keepdims=True)


def residual_sums(mates, stream, sums):
    count = len(stream)
    rows, cols = stream[0].shape
    whole = pl.BlockSpec(memory_space=pltpu.VMEM)
    return pl.pallas_call(
        functools.partial(residual_kernel, count),
        in_specs=[pl.BlockSpec(memory_space=pltpu.SMEM)] + [whole] * (count + len(sums)),
        out_specs=[whole] * 2,
        out_shape=[
            jax.ShapeDtypeStruct((count, rows, cols), F32),
            jax.ShapeDtypeStruct((count, rows, 1), F32),
        ],
        compiler_params=pltpu.CompilerParams(vmem_limit_bytes=32 * MIB),
    )(mates, *stream, *sums)


def hidden_kernel(sizes, groups, order_ref, *refs):
    steps = sum(sizes)
    each = len(sizes)
    pieces = [refs[g * each : (g + 1) * each] for g in range(groups)]
    refs = refs[groups * each :]
    scales, (gate_ref, up_ref), outs = refs[:groups], refs[groups : groups + 2], refs[groups + 2 :]
    outs, g_acc, u_acc = outs[:groups], outs[-2], outs[-1]
    i = pl.program_id(0)
    hid = gate_ref.shape[1]
    main = hid - 128 if hid % 256 == 128 else hid

    def products(rows):
        for acc, ref in ((g_acc, gate_ref), (u_acc, up_ref)):
            yield acc, slice(0, main), jnp.dot(rows, ref[:, :main], preferred_element_type=F32)
        if main < hid:
            rest = jnp.concatenate([gate_ref[:, main:], up_ref[:, main:]], axis=1)
            both = jnp.dot(rows, rest, preferred_element_type=F32)
            yield g_acc, slice(main, hid), both[:, : hid - main]
            yield u_acc, slice(main, hid), both[:, hid - main :]

    start = 0
    for p, size in enumerate(sizes):

        @pl.when((i >= start) & (i < start + size))
        def _(p=p, start=start):
            for g in range(groups):
                rows = pieces[g][p][0]
                for acc, at, product in products(rows):
                    if start == 0:
                        acc[g, :, at] = product
                    else:
                        acc[g, :, at] += product

        start += size

    @pl.when(i == steps - 1)
    def _():
        for g in range(groups):
            scale = scales[g][...]
            v = g_acc[g] * scale
            outs[g][...] = (v / (1.0 + jnp.exp(-v)) * (u_acc[g] * scale)).astype(BF)


def hidden_units(groups, scales, w_gate, w_up, order):
    sizes = [p.shape[0] for p in groups[0]]
    rows, cols = groups[0][0].shape[1:]
    depth, hid = w_gate.shape
    many = len(groups)
    specs = []
    start = 0
    for size in sizes:
        specs.append(
            pl.BlockSpec(
                (1, rows, cols),
                lambda i, order, start=start, size=size: (jnp.clip(i - start, 0, size - 1), 0, 0),
            )
        )
        start += size
    up_spec = pl.BlockSpec((cols, hid), lambda i, order: (order[i], 0))
    return pl.pallas_call(
        functools.partial(hidden_kernel, sizes, many),
        grid_spec=pltpu.PrefetchScalarGridSpec(
            num_scalar_prefetch=1,
            grid=(sum(sizes),),
            in_specs=specs * many
            + [pl.BlockSpec((rows, 1), lambda i, order: (0, 0))] * many
            + [up_spec, up_spec],
            out_specs=[pl.BlockSpec((rows, hid), lambda i, order: (0, 0))] * many,
            scratch_shapes=[pltpu.VMEM((many, rows, hid), F32)] * 2,
        ),
        out_shape=[jax.ShapeDtypeStruct((rows, hid), BF)] * many,
        compiler_params=pltpu.CompilerParams(vmem_limit_bytes=60 * MIB),
        cost_estimate=pl.CostEstimate(
            flops=8 * many * rows * depth * hid,
            bytes_accessed=4 * depth * hid + 2 * many * rows * depth,
            transcendentals=many * rows * hid,
        ),
    )(order, *[p for pieces in groups for p in pieces], *scales, w_gate, w_up)


def down_kernel(groups, order_ref, *refs):
    hidden, weight, outs = refs[:groups], refs[groups], refs[groups + 1 :]
    for g in range(groups):
        outs[g][0] = jnp.dot(hidden[g][...], weight[...], preferred_element_type=F32).astype(BF)


def down_blocks(hidden, w_down, order):
    many = len(hidden)
    rows, hid = hidden[0].shape
    blocks, model = order.shape[0], w_down.shape[1]
    cols = model // lax.axis_size("ctx")

    return pl.pallas_call(
        functools.partial(down_kernel, many),
        grid_spec=pltpu.PrefetchScalarGridSpec(
            num_scalar_prefetch=1,
            grid=(blocks,),
            in_specs=[pl.BlockSpec((rows, hid), lambda i, order: (0, 0))] * many
            + [pl.BlockSpec((hid, cols), lambda i, order: (0, order[i]))],
            out_specs=[pl.BlockSpec((1, rows, cols), lambda i, order: (i, 0, 0))] * many,
        ),
        out_shape=[jax.ShapeDtypeStruct((blocks, rows, cols), BF)] * many,
        compiler_params=pltpu.CompilerParams(vmem_limit_bytes=60 * MIB),
        cost_estimate=pl.CostEstimate(
            flops=4 * many * rows * cols * blocks * hid,
            bytes_accessed=2 * cols * blocks * hid + 2 * many * rows * cols * blocks,
            transcendentals=0,
        ),
    )(order, *hidden, w_down)


def body(
    queries,
    keys,
    values,
    decay_log,
    out_gate,
    head_gain,
    out_weight,
    stream,
    norm_gain,
    expert_ids,
    expert_share,
    w_gate,
    w_up,
    w_down,
):
    count = lax.axis_size("ctx")
    parts = lax.axis_size("exp")
    me = lax.axis_index("ctx")
    mine = lax.axis_index("exp")
    side = me & 1
    seqs, block, width = queries.shape
    heads = decay_log.shape[1]
    sub, model = stream.shape[1:]
    tokens = seqs * sub
    cols = model // count
    order = block_order(count, me)
    order_array = jnp.stack(order).astype(jnp.int32)

    cum = jnp.cumsum(decay_log, axis=0)
    small = jnp.concatenate(
        [
            expert_ids.reshape(2 * tokens).astype(F32),
            expert_share.reshape(2 * tokens),
            cum[-1],
        ]
    )
    cum_mine = lax.dynamic_slice_in_dim(cum, side * (heads // 2), heads // 2, 1)
    cum_theirs = lax.dynamic_slice_in_dim(cum, (1 - side) * (heads // 2), heads // 2, 1)
    halves = 2
    each = seqs // halves
    state_theirs = local_states(keys, values, cum_theirs, 1 - side, 0, each)
    small = jnp.pad(small, (0, -small.shape[0] % 128)).reshape(-1, 128)
    facts = joined(spread(after(small, state_theirs), count)).reshape(count, -1)
    steps = len(routes(count)[0])
    place = order_array[None, :] == jnp.arange(count, dtype=jnp.int32)[:, None]
    facts = jnp.sum(jnp.where(place[:, :, None], facts[None], 0.0), axis=1)
    ids = facts[:, : 2 * tokens].astype(jnp.int32)
    shares = facts[:, 2 * tokens : 4 * tokens]
    ends = facts[:, 4 * tokens : 4 * tokens + heads]

    mates = (me ^ jnp.arange(count, dtype=jnp.int32)).astype(jnp.int32)

    block_no = jnp.arange(count)

    def faded(source, target):
        between = (block_no >= 2 * (source // 2 + 1)) & (block_no < 2 * (target // 2))
        power = jnp.sum(jnp.where(between[:, None], ends, 0.0), axis=0)
        return jnp.where(source // 2 < target // 2, jnp.exp(power), 0.0)

    half_heads = heads // 2

    def side_half(row):
        return lax.dynamic_slice_in_dim(row, side * half_heads, half_heads, 0)

    fade_own = jnp.exp(cum[-1])
    lanes = jnp.pad(cum[-1:], ((0, 0), (0, -heads % 128)))
    fade_other = jnp.exp(send(lanes, pair(count))[0, :heads])
    ones = jnp.ones_like(fade_own)
    chip_weights = jnp.stack(
        [
            side_half(jnp.where(side == 0, fade_other, ones)),
            side_half(jnp.where(side == 0, ones, fade_own)),
        ]
    )
    enter_weights = jnp.stack(
        [jnp.where(side == 0, ones, fade_other), jnp.where(side == 0, 0.0, ones)]
    )

    there = me ^ hop_mask(count, steps - 1, side)
    summed = []
    arrivals, mixed, spreads = (), None, ()
    for h in range(halves):
        first = h * each
        if h:
            state_theirs = local_states(
                keys, values, after(cum_theirs, *arrivals[:1]), 1 - side, first, each
            )
        state_mine = local_states(
            keys, values, after(cum_mine, *arrivals[:1]), side, first, each
        )
        other_mine = send(state_theirs, pair(count))
        other_theirs = send(state_mine, pair(count))
        chip = combine([state_mine, other_mine], chip_weights)
        within, act = within_block(
            queries,
            keys,
            values,
            out_gate,
            after(cum, chip if mixed is None else mixed),
            head_gain,
            first,
            each,
        )
        held, names = [after(chip, *arrivals[1:])], [me]
        for step in range(steps - 1):
            got = send(jnp.stack(held) if step else held[0][None], hop(count, step))
            mask = hop_mask(count, step, side)
            held = held + [got[i] for i in range(len(held))]
            names = names + [name ^ mask for name in names]
        towards = [jnp.stack([side_half(faded(name, t)) for name in names]) for t in (there, me)]
        leaving = combine(held, after(towards[0], within, *spreads[1:2]))
        got = send(leaving, hop(count, steps - 1))
        arrivals = (held[-1], got)
        alone = jnp.concatenate([towards[1], jnp.ones((1, half_heads), F32)])
        entering = combine(held + [got], alone)
        states = [entering, send(entering, pair(count)), other_mine, other_theirs]
        mixed = mixed_rows(
            queries, states, enter_weights, side, within, act, cum, sub, first, each
        )
        gates = [spreads[2:3]] + [()] * (steps - 1) + [(partial,)] if h else ()
        pieces = spread(mixed.reshape(parts * each * sub, width), count, gates)
        partial = project(pieces, out_weight, order_array, parts)
        spreads = tuple(pieces)
        summed.append(lax.psum_scatter(partial, "exp", scatter_dimension=0))

    stream_rows = after(stream, partial).reshape(tokens, model)
    stream_got = swap_blocks(cut_columns(stream_rows, mates), count)
    residual, square = residual_sums(mates, stream_got, summed)
    residual = residual.reshape(count * tokens, cols)

    square = sum_over(square.reshape(count * tokens), count)
    scale = lax.rsqrt(square / model + 1e-06)
    gain = lax.dynamic_slice_in_dim(norm_gain, me * cols, cols, 0)
    rows_in = (residual * gain).astype(BF)

    expert_local = w_gate.shape[0]
    experts = expert_local * parts
    capacity = max(2, (2 * tokens + experts - 1) // experts + 1)
    one_hot = ids[:, :, None] == jnp.arange(experts, dtype=jnp.int32)
    earlier = jnp.arange(2 * tokens)[:, None] > jnp.arange(2 * tokens)[None, :]
    ahead = jnp.einsum(
        "tu,gue->gte", earlier.astype(BF), one_hot.astype(BF), preferred_element_type=F32
    )
    ranking = jnp.sum(jnp.where(one_hot, ahead, 0.0), axis=2).astype(jnp.int32)
    slots = capacity * count
    turned = (ids - mine + experts) % experts
    slot_of = (turned * count + jnp.arange(count, dtype=jnp.int32)[:, None]) * capacity + ranking
    slot_of = slot_of.reshape(count * tokens, 2)
    share_of = shares.reshape(count * tokens, 2)
    turns = [*range(0, parts, 2), *range(1, parts, 2)]
    sent, scales = [], []
    for turn in turns:
        numbers = turn * slots + jnp.arange(slots, dtype=jnp.int32)
        hit = [slot_of[:, k][None, :] == numbers[:, None] for k in range(2)]
        placing = hit[0] | hit[1]
        dispatch = jnp.dot(placing.astype(BF), rows_in, preferred_element_type=F32).astype(BF)
        slot_scale = jnp.sum(jnp.where(placing, scale[None, :], 0.0), axis=1)
        if turn:
            forth = [(i, (i + turn) % parts) for i in range(parts)]
            dispatch = lax.ppermute(dispatch, "exp", forth)
            slot_scale = lax.ppermute(slot_scale, "exp", forth)
        sent.append(dispatch)
        scales.append(slot_scale)

    arrived = []
    for turn in range(parts):
        gates = [()] * steps
        if turn == 0:
            gates[-1] = (sent[1], scale)
        elif turn == 1:
            gates[-1] = (arrived[0][steps], sent[2 % parts], *scales)
            gates.append((sent[3 % parts],))
        else:
            gates[0] = (arrived[0 if turn < 4 else turn - 2][steps],)
        arrived.append(spread(sent[turn], count, gates))
    near_order, far_order = order_array[: count // 2], order_array[count // 2 :]
    returned = []
    waits, moved = [], [[]] * steps
    for first in range(0, parts, 2):
        now = range(first, min(first + 2, parts))
        later = range(first + 2, min(first + 4, parts))
        ready = [arrived[t][1] for t in later]
        groups = [arrived[t] for t in now]
        groups[0] = list(after(tuple(groups[0]), *waits, *ready))
        factors = [scales[t][:, None] for t in now]
        hidden = hidden_units(groups, factors, w_gate[0], w_up[0], order_array)
        ready = [arrived[t][steps] for t in later]
        far = down_blocks(after(tuple(hidden), *ready, *moved[0]), w_down[0], far_order)
        ready = [arrived[t][-1] for t in later]
        near = down_blocks(after(tuple(hidden), *far, *ready), w_down[0], near_order)
        totals = [pair_sum(n, f, count) for n, f in zip(near, far)]
        waits = [leaves for _, leaves in totals]
        before = tuple(moved[-1])
        moved = [[] for _ in range(steps)]
        for turn, total in zip(turns[first : first + 2], totals):
            done, got = gathered_sum(total, count, (before,))
            for step in range(steps):
                moved[step].append(got[step])
            if first + 2 >= parts:
                before = (got[0],)
            if turn:
                back = [((i + turn) % parts, i) for i in range(parts)]
                done = lax.ppermute(done, "exp", back)
            returned.append(done)
    result = residual
    for at, turn in enumerate(turns):
        numbers = turn * slots + jnp.arange(slots, dtype=jnp.int32)
        weighting = sum(
            jnp.where(slot_of[:, k][:, None] == numbers[None, :], share_of[:, k][:, None], 0.0)
            for k in range(2)
        )
        high = weighting.astype(BF)
        low = (weighting - high.astype(F32)).astype(BF)
        result = result + jnp.dot(high, returned[at], preferred_element_type=F32)
        result = result + jnp.dot(low, returned[at], preferred_element_type=F32)
    result = result.astype(BF).reshape(count, tokens, cols)
    blocks = [lax.dynamic_index_in_dim(result, me ^ j, 0, False) for j in range(count)]
    return lay_columns(swap_blocks(blocks, count), mates).reshape(seqs, sub, model)


def solution(mesh):
    return jax.shard_map(
        body,
        mesh=mesh,
        in_specs=(
            P(None, "ctx", "exp"),
            P(None, "ctx", "exp"),
            P(None, "ctx", "exp"),
            P("ctx", "exp"),
            P(None, "ctx", "exp"),
            P("exp"),
            P("exp", "ctx"),
            P(None, ("ctx", "exp"), None),
            P(),
            P(("ctx", "exp"), None, None),
            P(("ctx", "exp"), None, None),
            P("exp", None, "ctx"),
            P("exp", None, "ctx"),
            P("exp", "ctx", None),
        ),
        out_specs=P(None, ("ctx", "exp"), None),
        check_vma=False,
    )
```
